32 devices in a mesh: ctx: 8 (over y, x, core), tp: 4 (over z).
Axes of the slice: x: 2, y: 2, z: 4, core: 2. Of those that a mesh axis runs over, the one named last changes fastest.
Arguments:
- query: bfloat16 [2048, 4096], P('ctx', 'tp'), may hold values from -6 to 6
- keys: bfloat16 [2048, 4096], P('ctx', 'tp'), may hold values from -6 to 6
- values: bfloat16 [2048, 4096], P('ctx', 'tp'), may hold values from -6 to 6
- filt: float32 [2048, 4096], P('ctx', 'tp'), may hold values from -1 to 1
- direct: float32 [4096], P('tp'), may hold values from -4 to 4
- w_out: bfloat16 [4096, 4096], P('tp'), may hold values from -0.09375 to 0.09375
Outputs:
- output: bfloat16 [2048, 4096], P('ctx', 'tp')
The draws below stay inside these ranges and needn't reach their ends.
All inputs are finite; a program needn't handle non-finite values.
Results may differ from the reference program's by a relative error of at most 0.0049.
Values sent between devices are 32-bit elements; how exact they have to be, the bound alone decides.
No kernel may reach another device: no remote copies, remote signals or barrier semaphores. Data moves between devices by JAX's collectives and lax.ppermute only.
A program may use at most 128 MiB of HBM per device.

```python
import math
import jax
import jax.numpy as jnp
from jax import lax

D = 4096
TOKENS = 2048


def draw_filt(key, part):
    key = jax.random.fold_in(key, 7)
    key_rate = jax.random.fold_in(key, 1)
    key_taps = jax.random.fold_in(key, 2)
    key_floor = jax.random.fold_in(key, 3)
    low = math.log(30.0)
    high = math.log(4.0 * TOKENS)
    total = float(TOKENS)
    reach = jnp.exp(jax.random.uniform(key_rate, (D,), jnp.float32, low, high))
    floor_level = jnp.sqrt(jax.random.uniform(key_floor, (D,), jnp.float32, 10.0, 40.0) / total)
    places = jnp.arange(TOKENS, dtype=jnp.float32)[:, None]
    envelope = jnp.exp(-places / reach[None, :]) + floor_level[None, :]
    first_sum = jnp.expm1(-total / reach) / jnp.expm1(-1.0 / reach)
    second_sum = jnp.expm1(-2.0 * total / reach) / jnp.expm1(-2.0 / reach)
    energy = second_sum + 2.0 * floor_level * first_sum + floor_level * floor_level * total
    scale = 0.6 / jnp.sqrt(energy)
    taps = jnp.clip(jax.random.normal(key_taps, (TOKENS, D), jnp.float32), -6.0, 6.0)
    return (taps * envelope * scale[None, :]).astype(jnp.float32)


def block_scale(own_key, dims, shards, least, top_value):
    def one(dim, blocks):
        heights = jax.random.uniform(jax.random.fold_in(jax.random.fold_in(own_key, 6), dim), (blocks,), jnp.float32, least / len(shards), top_value / len(shards))
        return jnp.repeat(jnp.exp(heights), dims[dim] // blocks).reshape((-1,) + (1,) * (len(dims) - dim - 1))

    gain = one(*shards[0])
    for cut in shards[1:]:
        gain = gain * one(*cut)
    return gain


def noise(stream_key, shape, width, limit, shards=(), kind=jnp.bfloat16):
    entries = jax.random.normal(stream_key, shape, jnp.float32) * width
    if len(shards) > 0:
        entries = block_scale(stream_key, shape, shards, -0.22, 0.18) * entries
    return jnp.clip(entries, min=-limit, max=limit).astype(kind)


def setup_inputs(seed: int = 0) -> dict:
    key_list = jax.random.split(jax.random.key(seed), 7)
    return {
        "query": noise(key_list[0], (TOKENS, D), 1.0, 6.0, ((0, 8), (1, 4))),
        "keys": noise(key_list[1], (TOKENS, D), 1.0, 6.0, ((0, 8), (1, 4))),
        "values": noise(key_list[2], (TOKENS, D), 1.0, 6.0, ((0, 8), (1, 4))),
        "filt": draw_filt(jax.random.fold_in(key_list[6], 71), 0),
        "direct": noise(key_list[4], (D,), 0.3, 4.0, ((0, 4),), jnp.float32),
        "w_out": noise(key_list[5], (D, D), D ** -0.5, 0.09375, ((0, 4),)),
    }


def reference(query, keys, values, filt, direct, w_out):
    signal = keys.astype(jnp.float32) * values.astype(jnp.float32)
    block = math.gcd(D, 256)
    count = D // block
    sig_blocks = signal.T.reshape(count, block, TOKENS)
    flt_blocks = filt.T.reshape(count, block, TOKENS)

    def convolve(pair):
        spec = jnp.fft.rfft(pair[0], n=2 * TOKENS, axis=-1) * jnp.fft.rfft(pair[1], n=2 * TOKENS, axis=-1)
        return jnp.fft.irfft(spec, n=2 * TOKENS, axis=-1)[:, :TOKENS]

    conv = lax.map(convolve, (sig_blocks, flt_blocks)).reshape(D, TOKENS).T.astype(jnp.float32)
    gated = (query.astype(jnp.float32) * (conv + direct[None, :] * signal)).astype(jnp.bfloat16)
    return jnp.dot(gated, w_out, preferred_element_type=jnp.float32).astype(jnp.bfloat16)
```

```python
import functools
import math

import jax
import jax.numpy as jnp
import ml_dtypes
import numpy as np
from jax import lax
from jax.experimental import pallas as pl
from jax.experimental.pallas import tpu as pltpu
from jax.sharding import PartitionSpec as P

F32 = jnp.float32
BF16 = jnp.bfloat16
VMEM_LIMIT = 56 * 1024 * 1024


def halves(table):
    high = table.astype(ml_dtypes.bfloat16)
    low = (table - high.astype(np.float64)).astype(ml_dtypes.bfloat16)
    return high, low


def tables(block):
    freq = 2 * np.arange(block, dtype=np.int64) + 1
    place = np.arange(block, dtype=np.int64)
    angle = 2.0 * math.pi / (4 * block) * (freq[:, None] * place[None, :] % (4 * block))
    forward = np.concatenate([np.cos(angle), -np.sin(angle)], axis=0)
    high, low = halves(forward)
    ahead = np.concatenate([high, high, low], axis=1)
    high, low = halves(forward.T / block)
    back = np.concatenate([high, high, low], axis=1)
    return ahead, back


def split3(value):
    high = value.astype(BF16)
    low = (value - high.astype(F32)).astype(BF16)
    return jnp.concatenate([high, low, high], axis=0)


def pack_kernel(place_ref, keys_ref, values_ref, filt_ref, *refs):
    outs, turned_ref = refs[:-1], refs[-1]
    chans = keys_ref.shape[1] // len(outs)
    for group in range(len(outs)):
        cols = slice(group * chans, (group + 1) * chans)
        slot = group ^ place_ref[0]
        turned_ref[slot, :, :chans] = keys_ref[:, cols].astype(F32) * values_ref[:, cols].astype(F32)
        turned_ref[slot, :, chans:] = filt_ref[:, cols]
    for turn, out in zip(turns(len(outs)), outs):
        out[...] = turned_ref[turn]


def pack(place, keys, values, filt, count):
    rows, width = keys.shape
    step = math.gcd(rows, 128)
    spec = pl.BlockSpec((step, width), lambda i: (i, 0))
    wide = 2 * width // count
    return pl.pallas_call(
        pack_kernel,
        grid=(rows // step,),
        in_specs=[pl.BlockSpec(memory_space=pltpu.SMEM), spec, spec, spec],
        out_specs=[pl.BlockSpec((step, wide), lambda i: (i, 0))] * count,
        out_shape=[jax.ShapeDtypeStruct((rows, wide), F32)] * count,
        scratch_shapes=[pltpu.VMEM((count, step, wide), F32)],
        compiler_params=pltpu.CompilerParams(vmem_limit_bytes=VMEM_LIMIT),
    )(place, keys, values, filt)


def turns(count):
    return [0, 1] + sorted(range(2, count), key=lambda d: (d & 1 and bin(d >> 1).count("1") == 1, -bin(d >> 1).count("1"), d))


def swap(arrays):
    count = len(arrays)
    pairs = [[(i, i ^ d) for i in range(count)] for d in turns(count)]
    return [arrays[0]] + [lax.ppermute(arrays[j], "ctx", pairs[j]) for j in range(1, count)]


def forward_kernel(ahead_ref, *refs):
    for j, x in enumerate(refs[:-1]):
        refs[-1][j] = jnp.dot(ahead_ref[...], split3(x[...]), preferred_element_type=F32)


def forward(xs, ahead):
    rows, width = xs[0].shape
    whole = pl.BlockSpec(memory_space=pltpu.VMEM)
    return pl.pallas_call(
        forward_kernel,
        in_specs=[whole] * (1 + len(xs)),
        out_specs=whole,
        out_shape=jax.ShapeDtypeStruct((len(xs), 2 * rows, width), F32),
        compiler_params=pltpu.CompilerParams(vmem_limit_bytes=VMEM_LIMIT),
    )(ahead, *xs)


def conv_kernel(place_ref, early_ref, *refs):
    first = early_ref.shape[0]
    count = (len(refs) - 4 + first) // 2
    xs, (ahead_ref, back_ref) = refs[: count - first], refs[count - first : count - first + 2]
    outs, (spec_ref, mix_ref) = refs[count - first + 2 : -2], refs[-2:]
    rows, width = xs[0].shape
    chans = width // 2
    place = place_ref[0]

    order = turns(count)
    for j, turn in enumerate(order):
        if j < first:
            spec_ref[turn ^ place] = early_ref[j]
        else:
            x = xs[j - first]
            spec_ref[turn ^ place] = jnp.dot(ahead_ref[...], split3(x[...]), preferred_element_type=F32)

    step = 8
    parity = lax.broadcasted_iota(jnp.int32, (step, chans), 0) % 2
    sign = (1 - 2 * parity).astype(F32)

    def combine(i, carry):
        real = pl.ds(pl.multiple_of(i * step, step), step)
        imag = pl.ds(pl.multiple_of(rows + i * step, step), step)
        flt = []
        last = None
        for j in range(count):
            here = (spec_ref[j, real, chans:], spec_ref[j, imag, chans:])
            if last is None:
                flt.append(here)
            else:
                flt.append((here[0] - sign * last[1], here[1] + sign * last[0]))
            last = here
        sig = [(spec_ref[j, real, :chans], spec_ref[j, imag, :chans]) for j in range(count)]
        for j in range(count):
            re = None
            for s in range(j + 1):
                a, b = sig[s]
                c, d = flt[j - s]
                if re is None:
                    re, im = a * c - b * d, a * d + b * c
                else:
                    re, im = re + (a * c - b * d), im + (a * d + b * c)
            mix_ref[j, real] = re
            mix_ref[j, imag] = im
        return carry

    lax.fori_loop(0, rows // step, combine, 0)

    for j in range(0, count, 2):
        pair = jnp.concatenate([mix_ref[order[j] ^ place], mix_ref[order[j + 1] ^ place]], axis=1)
        part = jnp.dot(back_ref[...], split3(pair), preferred_element_type=F32)
        outs[j][...] = part[:, :chans]
        outs[j + 1][...] = part[:, chans:]


def convolve(place, xs):
    count = len(xs)
    rows, width = xs[0].shape
    chans = width // 2
    ahead, back = (jnp.asarray(table) for table in tables(rows))
    first = count // 2
    early = forward(xs[:first], ahead)
    whole = pl.BlockSpec(memory_space=pltpu.VMEM)
    return pl.pallas_call(
        conv_kernel,
        in_specs=[pl.BlockSpec(memory_space=pltpu.SMEM)] + [whole] * (count - first + 3),
        out_specs=[whole] * count,
        out_shape=[jax.ShapeDtypeStruct((rows, chans), F32)] * count,
        scratch_shapes=[
            pltpu.VMEM((count, 2 * rows, width), F32),
            pltpu.VMEM((count, 2 * rows, chans), F32),
        ],
        compiler_params=pltpu.CompilerParams(vmem_limit_bytes=VMEM_LIMIT),
    )(place, early, *xs[first:], ahead, back)


CHAINS = 2


def gate_kernel(place_ref, q_ref, k_ref, v_ref, direct_ref, far_ref, *refs):
    convs, (gated_ref, *firsts), conv_ref = refs[: -2 - CHAINS], refs[-2 - CHAINS : -1], refs[-1]
    rows, chans = convs[0].shape
    for turn, ref in zip(turns(len(convs)), convs):
        conv_ref[turn ^ place_ref[0]] = ref[...]
    for group in range(len(convs)):
        cols = slice(group * chans, (group + 1) * chans)
        signal = k_ref[:, cols].astype(F32) * v_ref[:, cols].astype(F32)
        inner = conv_ref[group] + direct_ref[:, cols] * signal
        gated_ref[:, cols] = (q_ref[:, cols].astype(F32) * inner).astype(BF16)
    width = far_ref.shape[1] // CHAINS
    for k, out in enumerate(firsts):
        cols = slice(k * width, (k + 1) * width)
        out[...] = jnp.dot(gated_ref[...], far_ref[:, cols], preferred_element_type=F32)


def gate(place, query, keys, values, direct, far, convs):
    rows, width = query.shape
    whole = pl.BlockSpec(memory_space=pltpu.VMEM)
    first = jax.ShapeDtypeStruct((rows, far.shape[1] // CHAINS), F32)
    out = pl.pallas_call(
        gate_kernel,
        in_specs=[pl.BlockSpec(memory_space=pltpu.SMEM)] + [whole] * (5 + len(convs)),
        out_specs=[whole] * (1 + CHAINS),
        out_shape=[jax.ShapeDtypeStruct((rows, width), BF16)] + [first] * CHAINS,
        scratch_shapes=[pltpu.VMEM((len(convs),) + convs[0].shape, F32)],
        compiler_params=pltpu.CompilerParams(vmem_limit_bytes=VMEM_LIMIT),
    )(place, query, keys, values, direct, far, *convs)
    return out[0], out[1:]


def column_block(array, index, size):
    width = array.shape[1] // size
    return lax.dynamic_slice_in_dim(array, jnp.clip(index, 0, size - 1) * width, width, 1)


def pass_on(up, down, step, size):
    rise = [(z, z + 1) for z in range(min(step, size - 1))]
    fall = [(z, z - 1) for z in range(max(size - step, 1), size)]
    up, down = lax.optimization_barrier((up, down))
    up = lax.ppermute(up, "tp", rise)
    down = lax.ppermute(down, "tp", fall)
    return up, down


def first_step(value, size):
    place = lax.axis_index("tp")
    if size == 2:
        return pass_on(value, value, 1, size)
    got = lax.ppermute(value, "tp", [(0, 1), (size - 1, size - 2)])
    return jnp.where(place == 1, got, 0.0), jnp.where(place == size - 2, got, 0.0)


def scatter_dot(lhs, rhs, first):
    size = lax.axis_size("tp")
    place = lax.axis_index("tp")
    rows, width = first[0].shape
    lhs, first = lax.optimization_barrier((lhs, first))
    sums = [first_step(value, size) for value in first]
    terms = jnp.dot(lhs, rhs, preferred_element_type=F32)

    def own(index, k):
        start = jnp.clip(index, 0, size - 1) * (width * CHAINS) + k * width
        return lax.dynamic_slice_in_dim(terms, start, width, 1)

    for step in range(2, size):
        for k in range(CHAINS):
            up = sums[k][0] + own(place + size - step, k)
            down = sums[k][1] + own(place - size + step, k)
            up, down, terms = lax.optimization_barrier((up, down, terms))
            sums[k] = pass_on(up, down, step, size)
    out = jnp.zeros((rows, width * CHAINS), BF16)
    for k in range(CHAINS):
        part = (own(place, k) + sums[k][0] + sums[k][1]).astype(BF16)
        out = lax.dynamic_update_slice(out, part, (0, k * width))
        out, terms = lax.optimization_barrier((out, terms))
    return out


def body(query, keys, values, filt, direct, w_out):
    count = lax.axis_size("ctx")
    size = lax.axis_size("tp")
    place = lax.axis_index("ctx").reshape(1)
    xs = swap(pack(place, keys, values, filt, count))
    far = column_block(w_out, jnp.where(lax.axis_index("tp") == 0, size - 1, 0), size)
    xs[0], far = lax.optimization_barrier((xs[0], far))
    convs = swap(convolve(place, xs))
    gated, first = gate(place, query, keys, values, direct.reshape(1, -1), far, convs)
    return scatter_dot(gated, w_out, first)


def solution(mesh):
    return jax.shard_map(
        body,
        mesh=mesh,
        in_specs=(
            P("ctx", "tp"),
            P("ctx", "tp"),
            P("ctx", "tp"),
            P("ctx", "tp"),
            P("tp"),
            P("tp", None),
        ),
        out_specs=P("ctx", "tp"),
        check_vma=False,
    )
```

```python
import functools
import math

import jax
import jax.numpy as jnp
import ml_dtypes
import numpy as np
from jax import lax
from jax.experimental import pallas as pl
from jax.experimental.pallas import tpu as pltpu
from jax.sharding import PartitionSpec as P

F32 = jnp.float32
BF16 = jnp.bfloat16


def room(*shapes):
    total = 0
    for shape in shapes:
        lanes = -(-shape[-1] // 128) * 128
        total += 4 * lanes * math.prod(shape[:-1])
    return pltpu.CompilerParams(vmem_limit_bytes=total + total // 4 + 4 * 1024 * 1024)


def halves(table):
    high = table.astype(ml_dtypes.bfloat16)
    low = (table - high.astype(np.float64)).astype(ml_dtypes.bfloat16)
    return high, low


def tables(block):
    freq = 2 * np.arange(block, dtype=np.int64) + 1
    place = np.arange(block, dtype=np.int64)
    angle = 2.0 * math.pi / (4 * block) * (freq[:, None] * place[None, :] % (4 * block))
    forward = np.concatenate([np.cos(angle), -np.sin(angle)], axis=0)
    high, low = halves(forward)
    ahead = np.concatenate([high, high, low], axis=1)
    high, low = halves(forward.T / block)
    back = np.concatenate([high, high, low], axis=1)
    return ahead, back


def split3(value):
    high = value.astype(BF16)
    low = (value - high.astype(F32)).astype(BF16)
    return jnp.concatenate([high, low, high], axis=0)


def pack_kernel(place_ref, keys_ref, values_ref, filt_ref, *refs):
    outs, turned_ref = refs[:-1], refs[-1]
    chans = keys_ref.shape[1] // len(outs)
    for group in range(len(outs)):
        cols = slice(group * chans, (group + 1) * chans)
        slot = group ^ place_ref[0]
        turned_ref[slot, :, :chans] = keys_ref[:, cols].astype(F32) * values_ref[:, cols].astype(F32)
        turned_ref[slot, :, chans:] = filt_ref[:, cols]
    for turn, out in zip(turns(len(outs)), outs):
        out[...] = turned_ref[turn]


def pack(place, keys, values, filt, count):
    rows, width = keys.shape
    step = math.gcd(rows, 128)
    spec = pl.BlockSpec((step, width), lambda i: (i, 0))
    wide = 2 * width // count
    return pl.pallas_call(
        pack_kernel,
        grid=(rows // step,),
        in_specs=[pl.BlockSpec(memory_space=pltpu.SMEM), spec, spec, spec],
        out_specs=[pl.BlockSpec((step, wide), lambda i: (i, 0))] * count,
        out_shape=[jax.ShapeDtypeStruct((rows, wide), F32)] * count,
        scratch_shapes=[pltpu.VMEM((count, step, wide), F32)],
        compiler_params=pltpu.CompilerParams(vmem_limit_bytes=56 * 1024 * 1024),
    )(place, keys, values, filt)


def turns(count):
    return [0, 1] + sorted(range(2, count), key=lambda d: (d & 1 and bin(d >> 1).count("1") == 1, -bin(d >> 1).count("1"), d))


def swap(arrays):
    count = len(arrays)
    pairs = [[(i, i ^ d) for i in range(count)] for d in turns(count)]
    return [arrays[0]] + [lax.ppermute(arrays[j], "ctx", pairs[j]) for j in range(1, count)]


def forward_kernel(ahead_ref, *refs):
    for j, x in enumerate(refs[:-1]):
        refs[-1][j] = jnp.dot(ahead_ref[...], split3(x[...]), preferred_element_type=F32)


def forward(xs, ahead):
    rows, width = xs[0].shape
    whole = pl.BlockSpec(memory_space=pltpu.VMEM)
    return pl.pallas_call(
        forward_kernel,
        in_specs=[whole] * (1 + len(xs)),
        out_specs=whole,
        out_shape=jax.ShapeDtypeStruct((len(xs), 2 * rows, width), F32),
        compiler_params=room((len(xs), 2 * rows, width), (len(xs), rows, width), (4 * rows, 3 * rows)),
    )(ahead, *xs)


def conv_kernel(place_ref, early_ref, *refs):
    first = early_ref.shape[0]
    count = (len(refs) - 6 + first) // 2
    xs, (ahead_ref, back_hbm) = refs[: count - first], refs[count - first : count - first + 2]
    outs, (spec_ref, mix_ref, back_ref, back_sem) = refs[count - first + 2 : -4], refs[-4:]
    back_in = pltpu.make_async_copy(back_hbm, back_ref, back_sem)
    back_in.start()
    rows, width = xs[0].shape
    chans = width // 2
    place = place_ref[0]

    order = turns(count)
    for j, turn in enumerate(order):
        if j < first:
            spec_ref[turn ^ place] = early_ref[j]
        else:
            x = xs[j - first]
            spec_ref[turn ^ place] = jnp.dot(ahead_ref[...], split3(x[...]), preferred_element_type=F32)

    step = 8
    parity = lax.broadcasted_iota(jnp.int32, (step, chans), 0) % 2
    sign = (1 - 2 * parity).astype(F32)

    def combine(i, carry):
        real = pl.ds(pl.multiple_of(i * step, step), step)
        imag = pl.ds(pl.multiple_of(rows + i * step, step), step)
        sig = [(spec_ref[j, real, :chans], spec_ref[j, imag, :chans]) for j in range(count)]
        sums = [None] * count
        last = None
        for lag in range(count):
            here = (spec_ref[lag, real, chans:], spec_ref[lag, imag, chans:])
            c, d = here
            if last is not None:
                c, d = c - sign * last[1], d + sign * last[0]
            last = here
            for j in range(lag, count):
                a, b = sig[j - lag]
                re, im = a * c - b * d, a * d + b * c
                sums[j] = (re, im) if lag == 0 else (sums[j][0] + re, sums[j][1] + im)
        for j in range(count):
            mix_ref[j, real], mix_ref[j, imag] = sums[j]
        return carry

    lax.fori_loop(0, rows // step, combine, 0)

    back_in.wait()
    for j in range(0, count, 2):
        pair = jnp.concatenate([mix_ref[order[j] ^ place], mix_ref[order[j + 1] ^ place]], axis=1)
        part = jnp.dot(back_ref[...], split3(pair), preferred_element_type=F32)
        outs[j][...] = part[:, :chans]
        outs[j + 1][...] = part[:, chans:]


def convolve(place, xs):
    count = len(xs)
    rows, width = xs[0].shape
    chans = width // 2
    ahead, back = (jnp.asarray(table) for table in tables(rows))
    first = count // 2
    early = forward(xs[:first], ahead)
    whole = pl.BlockSpec(memory_space=pltpu.VMEM)
    return pl.pallas_call(
        conv_kernel,
        in_specs=[pl.BlockSpec(memory_space=pltpu.SMEM)]
        + [whole] * (count - first + 2)
        + [pl.BlockSpec(memory_space=pl.ANY)],
        out_specs=[whole] * count,
        out_shape=[jax.ShapeDtypeStruct((rows, chans), F32)] * count,
        scratch_shapes=[
            pltpu.VMEM((count, 2 * rows, width), F32),
            pltpu.VMEM((count, 2 * rows, chans), F32),
            pltpu.VMEM(back.shape, BF16),
            pltpu.SemaphoreType.DMA,
        ],
        compiler_params=room(
            *[(count, 2 * rows, width)] * 2, *[(count, 2 * rows, chans)] * 2, (4 * rows, 3 * rows)
        ),
    )(place, early, *xs[first:], ahead, back)


CHAINS = 2


def gate_kernel(place_ref, direct_ref, q_hbm, k_hbm, v_hbm, far_hbm, *refs):
    count = len(refs) - 10 - CHAINS
    convs, gated_hbm, firsts = refs[:count], refs[count], refs[count + 1 : -9]
    q_ref, k_ref, v_ref, far_ref, conv_ref, gated_ref, first_ref, in_sem, out_sem = refs[-9:]
    chans = convs[0].shape[1]
    width = far_ref.shape[1] // CHAINS

    into = [
        pltpu.make_async_copy(conv, conv_ref.at[turn ^ place_ref[0]], in_sem.at[4 + j])
        for j, (turn, conv) in enumerate(zip(turns(count), convs))
    ]
    pairs = ((q_hbm, q_ref), (k_hbm, k_ref), (v_hbm, v_ref), (far_hbm, far_ref))
    into += [pltpu.make_async_copy(src, dst, in_sem.at[j]) for j, (src, dst) in enumerate(pairs)]
    for copy in into:
        copy.start()
    for copy in into[:-1]:
        copy.wait()
    for group in range(count):
        cols = slice(group * chans, (group + 1) * chans)
        signal = k_ref[:, cols].astype(F32) * v_ref[:, cols].astype(F32)
        inner = conv_ref[group] + direct_ref[:, cols] * signal
        gated_ref[:, cols] = (q_ref[:, cols].astype(F32) * inner).astype(BF16)
    away = [pltpu.make_async_copy(gated_ref, gated_hbm, out_sem.at[CHAINS])]
    away[0].start()
    into[-1].wait()
    for k, out in enumerate(firsts):
        cols = slice(k * width, (k + 1) * width)
        first_ref[k] = jnp.dot(gated_ref[...], far_ref[:, cols], preferred_element_type=F32)
        away.append(pltpu.make_async_copy(first_ref.at[k], out, out_sem.at[k]))
        away[-1].start()
    for copy in away:
        copy.wait()


def gate(place, query, keys, values, direct, far, convs):
    rows, width = query.shape
    count = len(convs)
    there = pl.BlockSpec(memory_space=pl.ANY)
    part = (rows, far.shape[1] // CHAINS)
    blocks = (count,) + convs[0].shape
    out = pl.pallas_call(
        gate_kernel,
        in_specs=[pl.BlockSpec(memory_space=pltpu.SMEM), pl.BlockSpec(memory_space=pltpu.VMEM)]
        + [there] * (4 + count),
        out_specs=[there] * (1 + CHAINS),
        out_shape=[jax.ShapeDtypeStruct((rows, width), BF16)]
        + [jax.ShapeDtypeStruct(part, F32)] * CHAINS,
        scratch_shapes=[
            pltpu.VMEM((rows, width), BF16),
            pltpu.VMEM((rows, width), BF16),
            pltpu.VMEM((rows, width), BF16),
            pltpu.VMEM(far.shape, BF16),
            pltpu.VMEM(blocks, F32),
            pltpu.VMEM((rows, width), BF16),
            pltpu.VMEM((CHAINS,) + part, F32),
            pltpu.SemaphoreType.DMA((4 + count,)),
            pltpu.SemaphoreType.DMA((CHAINS + 1,)),
        ],
        compiler_params=pltpu.CompilerParams(vmem_limit_bytes=56 * 1024 * 1024),
    )(place, direct, query, keys, values, far, *convs)
    return out[0], out[1:]


def column_block(array, index, size):
    width = array.shape[1] // size
    return lax.dynamic_slice_in_dim(array, jnp.clip(index, 0, size - 1) * width, width, 1)


def pass_on(up, down, step, size):
    rise = [(z, z + 1) for z in range(min(step, size - 1))]
    fall = [(z, z - 1) for z in range(max(size - step, 1), size)]
    up, down = lax.optimization_barrier((up, down))
    up = lax.ppermute(up, "tp", rise)
    down = lax.ppermute(down, "tp", fall)
    return up, down


def first_step(value, size):
    place = lax.axis_index("tp")
    if size == 2:
        return pass_on(value, value, 1, size)
    got = lax.ppermute(value, "tp", [(0, 1), (size - 1, size - 2)])
    return jnp.where(place == 1, got, 0.0), jnp.where(place == size - 2, got, 0.0)


def scatter_dot(lhs, rhs, first):
    size = lax.axis_size("tp")
    place = lax.axis_index("tp")
    rows, width = first[0].shape
    lhs, first = lax.optimization_barrier((lhs, first))
    sums = [first_step(value, size) for value in first]
    terms = jnp.dot(lhs, rhs, preferred_element_type=F32)

    def own(index, k):
        start = jnp.clip(index, 0, size - 1) * (width * CHAINS) + k * width
        return lax.dynamic_slice_in_dim(terms, start, width, 1)

    for step in range(2, size):
        for k in range(CHAINS):
            up = sums[k][0] + own(place + size - step, k)
            down = sums[k][1] + own(place - size + step, k)
            up, down, terms = lax.optimization_barrier((up, down, terms))
            sums[k] = pass_on(up, down, step, size)
    out = jnp.zeros((rows, width * CHAINS), BF16)
    for k in range(CHAINS):
        part = (own(place, k) + sums[k][0] + sums[k][1]).astype(BF16)
        out = lax.dynamic_update_slice(out, part, (0, k * width))
        out, terms = lax.optimization_barrier((out, terms))
    return out


def body(query, keys, values, filt, direct, w_out):
    count = lax.axis_size("ctx")
    size = lax.axis_size("tp")
    place = lax.axis_index("ctx").reshape(1)
    xs = swap(pack(place, keys, values, filt, count))
    far = column_block(w_out, jnp.where(lax.axis_index("tp") == 0, size - 1, 0), size)
    xs[0], far = lax.optimization_barrier((xs[0], far))
    convs = swap(convolve(place, xs))
    gated, first = gate(place, query, keys, values, direct.reshape(1, -1), far, convs)
    return scatter_dot(gated, w_out, first)


def solution(mesh):
    return jax.shard_map(
        body,
        mesh=mesh,
        in_specs=(
            P("ctx", "tp"),
            P("ctx", "tp"),
            P("ctx", "tp"),
            P("ctx", "tp"),
            P("tp"),
            P("tp", None),
        ),
        out_specs=P("ctx", "tp"),
        check_vma=False,
    )
```

```python
import functools
import math

import jax
import jax.numpy as jnp
import ml_dtypes
import numpy as np
from jax import lax
from jax.experimental import pallas as pl
from jax.experimental.pallas import tpu as pltpu
from jax.sharding import PartitionSpec as P

F32 = jnp.float32
BF16 = jnp.bfloat16


def room(*shapes):
    total = 0
    for shape in shapes:
        lanes = -(-shape[-1] // 128) * 128
        total += 4 * lanes * math.prod(shape[:-1])
    return pltpu.CompilerParams(vmem_limit_bytes=total + total // 4 + 4 * 1024 * 1024)


def halves(table):
    high = table.astype(ml_dtypes.bfloat16)
    low = (table - high.astype(np.float64)).astype(ml_dtypes.bfloat16)
    return high, low


def tables(block):
    freq = 2 * np.arange(block, dtype=np.int64) + 1
    place = np.arange(block, dtype=np.int64)
    angle = 2.0 * math.pi / (4 * block) * (freq[:, None] * place[None, :] % (4 * block))
    forward = np.concatenate([np.cos(angle), -np.sin(angle)], axis=0)
    high, low = halves(forward)
    ahead = np.concatenate([high, high, low], axis=1)
    high, low = halves(forward.T / block)
    back = np.concatenate([high, high, low], axis=1)
    return ahead, back


def split3(value):
    high = value.astype(BF16)
    low = (value - high.astype(F32)).astype(BF16)
    return jnp.concatenate([high, low, high], axis=0)


def pack_kernel(place_ref, keys_ref, values_ref, filt_ref, direct_ref, *refs):
    outs, turned_ref = refs[:-1], refs[-1]
    chans = keys_ref.shape[1] // len(outs)
    origin = jnp.logical_and(place_ref[0] == 0, pl.program_id(0) == 0)
    rows = lax.broadcasted_iota(jnp.int32, (8, chans), 0)
    for group in range(len(outs)):
        cols = slice(group * chans, (group + 1) * chans)
        slot = group ^ place_ref[0]
        turned_ref[slot, :, :chans] = keys_ref[:, cols].astype(F32) * values_ref[:, cols].astype(F32)
        turned_ref[slot, :, chans:] = filt_ref[:, cols]
        here = jnp.where(jnp.logical_and(rows == 0, origin), direct_ref[:, cols], 0.0)
        turned_ref[slot, :8, chans:] = filt_ref[:8, cols] + here
    for turn, out in zip(turns(len(outs)), outs):
        out[...] = turned_ref[turn]


def pack(place, keys, values, filt, direct, count):
    rows, width = keys.shape
    step = math.gcd(rows, 128)
    spec = pl.BlockSpec((step, width), lambda i: (i, 0))
    wide = 2 * width // count
    return pl.pallas_call(
        pack_kernel,
        grid=(rows // step,),
        in_specs=[pl.BlockSpec(memory_space=pltpu.SMEM), spec, spec, spec]
        + [pl.BlockSpec((1, width), lambda i: (0, 0))],
        out_specs=[pl.BlockSpec((step, wide), lambda i: (i, 0))] * count,
        out_shape=[jax.ShapeDtypeStruct((rows, wide), F32)] * count,
        scratch_shapes=[pltpu.VMEM((count, step, wide), F32)],
        compiler_params=pltpu.CompilerParams(vmem_limit_bytes=56 * 1024 * 1024),
    )(place, keys, values, filt, direct)


def turns(count):
    return [0, 1] + sorted(range(2, count), key=lambda d: (d & 1 and bin(d >> 1).count("1") == 1, -bin(d >> 1).count("1"), d))


def swap(arrays):
    count = len(arrays)
    pairs = [[(i, i ^ d) for i in range(count)] for d in turns(count)]
    return [arrays[0]] + [lax.ppermute(arrays[j], "ctx", pairs[j]) for j in range(1, count)]


def forward_kernel(ahead_ref, *refs):
    for j, x in enumerate(refs[:-1]):
        refs[-1][j] = jnp.dot(ahead_ref[...], split3(x[...]), preferred_element_type=F32)


def forward(xs, ahead):
    rows, width = xs[0].shape
    whole = pl.BlockSpec(memory_space=pltpu.VMEM)
    return pl.pallas_call(
        forward_kernel,
        in_specs=[whole] * (1 + len(xs)),
        out_specs=whole,
        out_shape=jax.ShapeDtypeStruct((len(xs), 2 * rows, width), F32),
        compiler_params=room((len(xs), 2 * rows, width), (len(xs), rows, width), (4 * rows, 3 * rows)),
    )(ahead, *xs)


def conv_kernel(place_ref, early_ref, *refs):
    first = early_ref.shape[0]
    count = (len(refs) - 6 + first) // 2
    xs, (ahead_ref, back_hbm) = refs[: count - first], refs[count - first : count - first + 2]
    outs, (spec_ref, mix_ref, back_ref, back_sem) = refs[count - first + 2 : -4], refs[-4:]
    back_in = pltpu.make_async_copy(back_hbm, back_ref, back_sem)
    back_in.start()
    rows, width = xs[0].shape
    chans = width // 2
    place = place_ref[0]

    order = turns(count)
    for j, turn in enumerate(order):
        if j < first:
            spec_ref[turn ^ place] = early_ref[j]
        else:
            x = xs[j - first]
            spec_ref[turn ^ place] = jnp.dot(ahead_ref[...], split3(x[...]), preferred_element_type=F32)

    step = 8
    parity = lax.broadcasted_iota(jnp.int32, (step, chans), 0) % 2
    sign = (1 - 2 * parity).astype(F32)

    def combine(i, carry):
        real = pl.ds(pl.multiple_of(i * step, step), step)
        imag = pl.ds(pl.multiple_of(rows + i * step, step), step)
        sig = [(spec_ref[j, real, :chans], spec_ref[j, imag, :chans]) for j in range(count)]
        sums = [None] * count
        last = None
        for lag in range(count):
            here = (spec_ref[lag, real, chans:], spec_ref[lag, imag, chans:])
            c, d = here
            if last is not None:
                c, d = c - sign * last[1], d + sign * last[0]
            last = here
            for j in range(lag, count):
                a, b = sig[j - lag]
                re, im = a * c - b * d, a * d + b * c
                sums[j] = (re, im) if lag == 0 else (sums[j][0] + re, sums[j][1] + im)
        for j in range(count):
            mix_ref[j, real], mix_ref[j, imag] = sums[j]
        return carry

    lax.fori_loop(0, rows // step, combine, 0)

    back_in.wait()
    for j in range(0, count, 2):
        pair = jnp.concatenate([mix_ref[order[j] ^ place], mix_ref[order[j + 1] ^ place]], axis=1)
        part = jnp.dot(back_ref[...], split3(pair), preferred_element_type=F32)
        outs[j][...] = part[:, :chans]
        outs[j + 1][...] = part[:, chans:]


def convolve(place, xs):
    count = len(xs)
    rows, width = xs[0].shape
    chans = width // 2
    ahead, back = (jnp.asarray(table) for table in tables(rows))
    first = count // 2
    early = forward(xs[:first], ahead)
    whole = pl.BlockSpec(memory_space=pltpu.VMEM)
    return pl.pallas_call(
        conv_kernel,
        in_specs=[pl.BlockSpec(memory_space=pltpu.SMEM)]
        + [whole] * (count - first + 2)
        + [pl.BlockSpec(memory_space=pl.ANY)],
        out_specs=[whole] * count,
        out_shape=[jax.ShapeDtypeStruct((rows, chans), F32)] * count,
        scratch_shapes=[
            pltpu.VMEM((count, 2 * rows, width), F32),
            pltpu.VMEM((count, 2 * rows, chans), F32),
            pltpu.VMEM(back.shape, BF16),
            pltpu.SemaphoreType.DMA,
        ],
        compiler_params=room(
            (count, 2 * rows, width), *[(count, 2 * rows, chans)] * 2, (count, rows, width)
        ),
    )(place, early, *xs[first:], ahead, back)


CHAINS = 2


def gate_kernel(place_ref, far_ref, q_hbm, *refs):
    count = len(refs) - 4 - CHAINS
    convs, (gated_ref, *firsts), (q_ref, conv_ref, in_sem) = refs[:count], refs[count:-3], refs[-3:]
    chans = convs[0].shape[1]
    width = far_ref.shape[1] // CHAINS
    into = [pltpu.make_async_copy(q_hbm, q_ref, in_sem.at[count])]
    into += [
        pltpu.make_async_copy(conv, conv_ref.at[turn ^ place_ref[0]], in_sem.at[j])
        for j, (turn, conv) in enumerate(zip(turns(count), convs))
    ]
    for copy in into:
        copy.start()
    for copy in into:
        copy.wait()
    for group in range(count):
        cols = slice(group * chans, (group + 1) * chans)
        gated_ref[:, cols] = (q_ref[:, cols].astype(F32) * conv_ref[group]).astype(BF16)
    for k, out in enumerate(firsts):
        cols = slice(k * width, (k + 1) * width)
        out[...] = jnp.dot(gated_ref[...], far_ref[:, cols], preferred_element_type=F32)


def gate(place, query, far, convs):
    rows, width = query.shape
    count = len(convs)
    here = pl.BlockSpec(memory_space=pltpu.VMEM)
    there = pl.BlockSpec(memory_space=pl.ANY)
    part = (rows, far.shape[1] // CHAINS)
    blocks = (count,) + convs[0].shape
    out = pl.pallas_call(
        gate_kernel,
        in_specs=[pl.BlockSpec(memory_space=pltpu.SMEM), here] + [there] * (1 + count),
        out_specs=[here] * (1 + CHAINS),
        out_shape=[jax.ShapeDtypeStruct((rows, width), BF16)]
        + [jax.ShapeDtypeStruct(part, F32)] * CHAINS,
        scratch_shapes=[
            pltpu.VMEM((rows, width), BF16),
            pltpu.VMEM(blocks, F32),
            pltpu.SemaphoreType.DMA((count + 1,)),
        ],
        compiler_params=room(*[(rows, width)] * 2, far.shape, blocks, (CHAINS,) + part),
    )(place, far, query, *convs)
    return out[0], out[1:]


def column_block(array, index, size):
    width = array.shape[1] // size
    return lax.dynamic_slice_in_dim(array, jnp.clip(index, 0, size - 1) * width, width, 1)


def pass_on(up, down, step, size):
    rise = [(z, z + 1) for z in range(min(step, size - 1))]
    fall = [(z, z - 1) for z in range(max(size - step, 1), size)]
    up, down = lax.optimization_barrier((up, down))
    up = lax.ppermute(up, "tp", rise)
    down = lax.ppermute(down, "tp", fall)
    return up, down


def first_step(value, size):
    place = lax.axis_index("tp")
    if size == 2:
        return pass_on(value, value, 1, size)
    got = lax.ppermute(value, "tp", [(0, 1), (size - 1, size - 2)])
    return jnp.where(place == 1, got, 0.0), jnp.where(place == size - 2, got, 0.0)


def scatter_dot(lhs, rhs, first):
    size = lax.axis_size("tp")
    place = lax.axis_index("tp")
    rows, width = first[0].shape
    lhs, first = lax.optimization_barrier((lhs, first))
    sums = [first_step(value, size) for value in first]
    terms = jnp.dot(lhs, rhs, preferred_element_type=F32)

    def own(index, k):
        start = jnp.clip(index, 0, size - 1) * (width * CHAINS) + k * width
        return lax.dynamic_slice_in_dim(terms, start, width, 1)

    for step in range(2, size):
        for k in range(CHAINS):
            up = sums[k][0] + own(place + size - step, k)
            down = sums[k][1] + own(place - size + step, k)
            up, down, terms = lax.optimization_barrier((up, down, terms))
            sums[k] = pass_on(up, down, step, size)
    out = jnp.zeros((rows, width * CHAINS), BF16)
    for k in range(CHAINS):
        part = (own(place, k) + sums[k][0] + sums[k][1]).astype(BF16)
        out = lax.dynamic_update_slice(out, part, (0, k * width))
        out, terms = lax.optimization_barrier((out, terms))
    return out


def body(query, keys, values, filt, direct, w_out):
    count = lax.axis_size("ctx")
    size = lax.axis_size("tp")
    place = lax.axis_index("ctx").reshape(1)
    xs = swap(pack(place, keys, values, filt, direct.reshape(1, -1), count))
    far = column_block(w_out, jnp.where(lax.axis_index("tp") == 0, size - 1, 0), size)
    xs[0], far = lax.optimization_barrier((xs[0], far))
    convs = swap(convolve(place, xs))
    gated, first = gate(place, query, far, convs)
    return scatter_dot(gated, w_out, first)


def solution(mesh):
    return jax.shard_map(
        body,
        mesh=mesh,
        in_specs=(
            P("ctx", "tp"),
            P("ctx", "tp"),
            P("ctx", "tp"),
            P("ctx", "tp"),
            P("tp"),
            P("tp", None),
        ),
        out_specs=P("ctx", "tp"),
        check_vma=False,
    )
```

```python
import functools
import math

import jax
import jax.numpy as jnp
import ml_dtypes
import numpy as np
from jax import lax
from jax.experimental import pallas as pl
from jax.experimental.pallas import tpu as pltpu
from jax.sharding import PartitionSpec as P

F32 = jnp.float32
BF16 = jnp.bfloat16


def stay(array):
    return pltpu.with_memory_space_constraint(array, pltpu.MemorySpace.HBM)


def room(*shapes):
    total = 0
    for shape in shapes:
        lanes = -(-shape[-1] // 128) * 128
        total += 4 * lanes * math.prod(shape[:-1])
    return pltpu.CompilerParams(vmem_limit_bytes=total + total // 4 + 4 * 1024 * 1024)


def halves(table):
    high = table.astype(ml_dtypes.bfloat16)
    low = (table - high.astype(np.float64)).astype(ml_dtypes.bfloat16)
    return high, low


def tables(block):
    freq = 2 * np.arange(block, dtype=np.int64) + 1
    place = np.arange(block, dtype=np.int64)
    angle = 2.0 * math.pi / (4 * block) * (freq[:, None] * place[None, :] % (4 * block))
    forward = np.concatenate([np.cos(angle), -np.sin(angle)], axis=0)
    high, low = halves(forward)
    ahead = np.concatenate([high, high, low], axis=1)
    high, low = halves(forward.T / block)
    back = np.concatenate([high, high, low], axis=1)
    return ahead, back


def split3(value):
    high = value.astype(BF16)
    low = (value - high.astype(F32)).astype(BF16)
    return jnp.concatenate([high, low, high], axis=0)


def pack_kernel(place_ref, keys_ref, values_ref, filt_ref, direct_ref, *refs):
    outs, turned_ref = refs[:-1], refs[-1]
    chans = keys_ref.shape[1] // len(outs)
    origin = jnp.logical_and(place_ref[0] == 0, pl.program_id(0) == 0)
    rows = lax.broadcasted_iota(jnp.int32, (8, chans), 0)
    for group in range(len(outs)):
        cols = slice(group * chans, (group + 1) * chans)
        slot = group ^ place_ref[0]
        turned_ref[slot, :, :chans] = keys_ref[:, cols].astype(F32) * values_ref[:, cols].astype(F32)
        turned_ref[slot, :, chans:] = filt_ref[:, cols]
        here = jnp.where(jnp.logical_and(rows == 0, origin), direct_ref[:, cols], 0.0)
        turned_ref[slot, :8, chans:] = filt_ref[:8, cols] + here
    for turn, out in zip(turns(len(outs)), outs):
        out[...] = turned_ref[turn]


def pack(place, keys, values, filt, direct, count):
    rows, width = keys.shape
    step = math.gcd(rows, 128)
    spec = pl.BlockSpec((step, width), lambda i: (i, 0))
    wide = 2 * width // count
    return pl.pallas_call(
        pack_kernel,
        grid=(rows // step,),
        in_specs=[pl.BlockSpec(memory_space=pltpu.SMEM), spec, spec, spec]
        + [pl.BlockSpec((1, width), lambda i: (0, 0))],
        out_specs=[pl.BlockSpec((step, wide), lambda i: (i, 0))] * count,
        out_shape=[jax.ShapeDtypeStruct((rows, wide), F32)] * count,
        scratch_shapes=[pltpu.VMEM((count, step, wide), F32)],
        compiler_params=pltpu.CompilerParams(vmem_limit_bytes=56 * 1024 * 1024),
    )(place, stay(keys), stay(values), stay(filt), stay(direct))


def turns(count):
    return [0, 1] + sorted(range(2, count), key=lambda d: (d & 1 and bin(d >> 1).count("1") == 1, -bin(d >> 1).count("1"), d))


def swap(arrays):
    count = len(arrays)
    pairs = [[(i, i ^ d) for i in range(count)] for d in turns(count)]
    return [arrays[0]] + [lax.ppermute(arrays[j], "ctx", pairs[j]) for j in range(1, count)]


def forward_kernel(ahead_ref, *refs):
    for j, x in enumerate(refs[:-1]):
        refs[-1][j] = jnp.dot(ahead_ref[...], split3(x[...]), preferred_element_type=F32)


def forward(xs, ahead):
    rows, width = xs[0].shape
    whole = pl.BlockSpec(memory_space=pltpu.VMEM)
    return pl.pallas_call(
        forward_kernel,
        in_specs=[whole] * (1 + len(xs)),
        out_specs=whole,
        out_shape=jax.ShapeDtypeStruct((len(xs), 2 * rows, width), F32),
        compiler_params=room((len(xs), 2 * rows, width), (len(xs), rows, width), (4 * rows, 3 * rows)),
    )(ahead, *xs)


def conv_kernel(place_ref, early_ref, ahead_ref, back_hbm, *refs):
    first = early_ref.shape[0]
    spec_ref, mix_ref, x_ref, out_ref, back_ref, x_sem, out_sem, back_sem = refs[-8:]
    count = spec_ref.shape[0]
    xs, outs = refs[: count - first], refs[count - first : -8]
    rows, width = xs[0].shape
    chans = width // 2
    place = place_ref[0]
    order = turns(count)

    blocks_in = [pltpu.make_async_copy(x, x_ref.at[j], x_sem.at[j]) for j, x in enumerate(xs)]
    for copy in blocks_in:
        copy.start()
    back_in = pltpu.make_async_copy(back_hbm, back_ref, back_sem)
    back_in.start()
    for j, turn in enumerate(order):
        if j < first:
            spec_ref[turn ^ place] = early_ref[j]
        else:
            blocks_in[j - first].wait()
            spec_ref[turn ^ place] = jnp.dot(ahead_ref[...], split3(x_ref[j - first]), preferred_element_type=F32)

    step = 8
    parity = lax.broadcasted_iota(jnp.int32, (step, chans), 0) % 2
    sign = (1 - 2 * parity).astype(F32)

    def combine(i, carry):
        real = pl.ds(pl.multiple_of(i * step, step), step)
        imag = pl.ds(pl.multiple_of(rows + i * step, step), step)
        sig = [(spec_ref[j, real, :chans], spec_ref[j, imag, :chans]) for j in range(count)]
        sums = [None] * count
        last = None
        for lag in range(count):
            here = (spec_ref[lag, real, chans:], spec_ref[lag, imag, chans:])
            c, d = here
            if last is not None:
                c, d = c - sign * last[1], d + sign * last[0]
            last = here
            for j in range(lag, count):
                a, b = sig[j - lag]
                re, im = a * c - b * d, a * d + b * c
                sums[j] = (re, im) if lag == 0 else (sums[j][0] + re, sums[j][1] + im)
        for j in range(count):
            mix_ref[j, real], mix_ref[j, imag] = sums[j]
        return carry

    lax.fori_loop(0, rows // step, combine, 0)

    back_in.wait()
    blocks_out = [pltpu.make_async_copy(out_ref.at[j], out, out_sem.at[j]) for j, out in enumerate(outs)]
    for j in range(0, count, 2):
        pair = jnp.concatenate([mix_ref[order[j] ^ place], mix_ref[order[j + 1] ^ place]], axis=1)
        part = jnp.dot(back_ref[...], split3(pair), preferred_element_type=F32)
        out_ref[j] = part[:, :chans]
        out_ref[j + 1] = part[:, chans:]
        blocks_out[j].start()
        blocks_out[j + 1].start()
    for copy in blocks_out:
        copy.wait()


def convolve(place, xs):
    count = len(xs)
    rows, width = xs[0].shape
    chans = width // 2
    ahead, back = (jnp.asarray(table) for table in tables(rows))
    first = count // 2
    early = forward(xs[:first], ahead)
    whole = pl.BlockSpec(memory_space=pltpu.VMEM)
    there = pl.BlockSpec(memory_space=pl.ANY)
    scratch = [
        (count, 2 * rows, width),
        (count, 2 * rows, chans),
        (count - first, rows, width),
        (count, rows, chans),
    ]
    return pl.pallas_call(
        conv_kernel,
        in_specs=[pl.BlockSpec(memory_space=pltpu.SMEM), whole, whole] + [there] * (count - first + 1),
        out_specs=[there] * count,
        out_shape=[jax.ShapeDtypeStruct((rows, chans), F32)] * count,
        scratch_shapes=[pltpu.VMEM(shape, F32) for shape in scratch]
        + [
            pltpu.VMEM(back.shape, BF16),
            pltpu.SemaphoreType.DMA((count - first,)),
            pltpu.SemaphoreType.DMA((count,)),
            pltpu.SemaphoreType.DMA,
        ],
        compiler_params=room(*scratch, scratch[1]),
    )(place, early, ahead, stay(back), *xs[first:])


CHAINS = 2


def gate_kernel(place_ref, far_ref, q_hbm, *refs):
    count = len(refs) - 4 - CHAINS
    convs, (gated_ref, *firsts), (q_ref, conv_ref, in_sem) = refs[:count], refs[count:-3], refs[-3:]
    chans = convs[0].shape[1]
    width = far_ref.shape[1] // CHAINS
    into = [pltpu.make_async_copy(q_hbm, q_ref, in_sem.at[count])]
    into += [
        pltpu.make_async_copy(conv, conv_ref.at[turn ^ place_ref[0]], in_sem.at[j])
        for j, (turn, conv) in enumerate(zip(turns(count), convs))
    ]
    for copy in into:
        copy.start()
    for copy in into:
        copy.wait()
    for group in range(count):
        cols = slice(group * chans, (group + 1) * chans)
        gated_ref[:, cols] = (q_ref[:, cols].astype(F32) * conv_ref[group]).astype(BF16)
    for k, out in enumerate(firsts):
        cols = slice(k * width, (k + 1) * width)
        out[...] = jnp.dot(gated_ref[...], far_ref[:, cols], preferred_element_type=F32)


def gate(place, query, far, convs):
    rows, width = query.shape
    count = len(convs)
    here = pl.BlockSpec(memory_space=pltpu.VMEM)
    there = pl.BlockSpec(memory_space=pl.ANY)
    part = (rows, far.shape[1] // CHAINS)
    blocks = (count,) + convs[0].shape
    out = pl.pallas_call(
        gate_kernel,
        in_specs=[pl.BlockSpec(memory_space=pltpu.SMEM), here] + [there] * (1 + count),
        out_specs=[here] * (1 + CHAINS),
        out_shape=[pltpu.VMEM((rows, width), BF16)] + [pltpu.VMEM(part, F32)] * CHAINS,
        scratch_shapes=[
            pltpu.VMEM((rows, width), BF16),
            pltpu.VMEM(blocks, F32),
            pltpu.SemaphoreType.DMA((count + 1,)),
        ],
        compiler_params=room(*[(rows, width)] * 2, far.shape, blocks, (CHAINS,) + part),
    )(place, far, stay(query), *convs)
    return out[0], out[1:]


def column_block(array, index, size):
    width = array.shape[1] // size
    return lax.dynamic_slice_in_dim(array, jnp.clip(index, 0, size - 1) * width, width, 1)


def pass_on(up, down, step, size):
    rise = [(z, z + 1) for z in range(min(step, size - 1))]
    fall = [(z, z - 1) for z in range(max(size - step, 1), size)]
    up, down = lax.optimization_barrier((up, down))
    up = lax.ppermute(up, "tp", rise)
    down = lax.ppermute(down, "tp", fall)
    return up, down


def first_step(value, size):
    place = lax.axis_index("tp")
    if size == 2:
        return pass_on(value, value, 1, size)
    got = lax.ppermute(value, "tp", [(0, 1), (size - 1, size - 2)])
    return jnp.where(place == 1, got, 0.0), jnp.where(place == size - 2, got, 0.0)


def scatter_dot(lhs, rhs, first):
    size = lax.axis_size("tp")
    place = lax.axis_index("tp")
    rows, width = first[0].shape
    lhs, first = lax.optimization_barrier((lhs, first))
    sums = [first_step(value, size) for value in first]
    terms = jnp.dot(lhs, rhs, preferred_element_type=F32)

    def own(index, k):
        start = jnp.clip(index, 0, size - 1) * (width * CHAINS) + k * width
        return lax.dynamic_slice_in_dim(terms, start, width, 1)

    for step in range(2, size):
        for k in range(CHAINS):
            up = sums[k][0] + own(place + size - step, k)
            down = sums[k][1] + own(place - size + step, k)
            up, down, terms = lax.optimization_barrier((up, down, terms))
            sums[k] = pass_on(up, down, step, size)
    out = jnp.zeros((rows, width * CHAINS), BF16)
    for k in range(CHAINS):
        part = (own(place, k) + sums[k][0] + sums[k][1]).astype(BF16)
        out = lax.dynamic_update_slice(out, part, (0, k * width))
        out, terms = lax.optimization_barrier((out, terms))
    return out


def body(query, keys, values, filt, direct, w_out):
    count = lax.axis_size("ctx")
    size = lax.axis_size("tp")
    place = lax.axis_index("ctx").reshape(1)
    xs = swap(pack(place, keys, values, filt, direct.reshape(1, -1), count))
    far = column_block(w_out, jnp.where(lax.axis_index("tp") == 0, size - 1, 0), size)
    xs[0], far = lax.optimization_barrier((xs[0], far))
    convs = swap(convolve(place, xs))
    gated, first = gate(place, query, far, convs)
    return scatter_dot(gated, w_out, first)


def solution(mesh):
    return jax.shard_map(
        body,
        mesh=mesh,
        in_specs=(
            P("ctx", "tp"),
            P("ctx", "tp"),
            P("ctx", "tp"),
            P("ctx", "tp"),
            P("tp"),
            P("tp", None),
        ),
        out_specs=P("ctx", "tp"),
        check_vma=False,
    )
```

```python
import functools
import math

import jax
import jax.numpy as jnp
import ml_dtypes
import numpy as np
from jax import lax
from jax.experimental import pallas as pl
from jax.experimental.pallas import tpu as pltpu
from jax.sharding import PartitionSpec as P

F32 = jnp.float32
BF16 = jnp.bfloat16


def stay(array):
    return pltpu.with_memory_space_constraint(array, pltpu.MemorySpace.HBM)


def room(*shapes):
    total = 0
    for shape in shapes:
        lanes = -(-shape[-1] // 128) * 128
        total += 4 * lanes * math.prod(shape[:-1])
    return pltpu.CompilerParams(vmem_limit_bytes=total + total // 4 + 4 * 1024 * 1024)


def halves(table):
    high = table.astype(ml_dtypes.bfloat16)
    low = (table - high.astype(np.float64)).astype(ml_dtypes.bfloat16)
    return high, low


def tables(block):
    freq = 2 * np.arange(block, dtype=np.int64) + 1
    place = np.arange(block, dtype=np.int64)
    angle = 2.0 * math.pi / (4 * block) * (freq[:, None] * place[None, :] % (4 * block))
    forward = np.concatenate([np.cos(angle), -np.sin(angle)], axis=0)
    high, low = halves(forward)
    ahead = np.concatenate([high, high, low], axis=1)
    high, low = halves(forward.T / block)
    back = np.concatenate([high, high, low], axis=1)
    return ahead, back


def split3(value):
    high = value.astype(BF16)
    low = (value - high.astype(F32)).astype(BF16)
    return jnp.concatenate([high, low, high], axis=0)


def pack_kernel(place_ref, keys_ref, values_ref, filt_ref, direct_ref, *refs):
    outs, turned_ref = refs[:-1], refs[-1]
    chans = keys_ref.shape[1] // len(outs)
    origin = jnp.logical_and(place_ref[0] == 0, pl.program_id(0) == 0)
    rows = lax.broadcasted_iota(jnp.int32, (8, chans), 0)
    for group in range(len(outs)):
        cols = slice(group * chans, (group + 1) * chans)
        slot = group ^ place_ref[0]
        turned_ref[slot, :, :chans] = keys_ref[:, cols].astype(F32) * values_ref[:, cols].astype(F32)
        turned_ref[slot, :, chans:] = filt_ref[:, cols]
        here = jnp.where(jnp.logical_and(rows == 0, origin), direct_ref[:, cols], 0.0)
        turned_ref[slot, :8, chans:] = filt_ref[:8, cols] + here
    for turn, out in zip(turns(len(outs)), outs):
        out[...] = turned_ref[turn]


def pack(place, keys, values, filt, direct, count):
    rows, width = keys.shape
    step = math.gcd(rows, 128)
    spec = pl.BlockSpec((step, width), lambda i: (i, 0))
    wide = 2 * width // count
    return pl.pallas_call(
        pack_kernel,
        grid=(rows // step,),
        in_specs=[pl.BlockSpec(memory_space=pltpu.SMEM), spec, spec, spec]
        + [pl.BlockSpec((1, width), lambda i: (0, 0))],
        out_specs=[pl.BlockSpec((step, wide), lambda i: (i, 0))] * count,
        out_shape=[jax.ShapeDtypeStruct((rows, wide), F32)] * count,
        scratch_shapes=[pltpu.VMEM((count, step, wide), F32)],
        compiler_params=pltpu.CompilerParams(vmem_limit_bytes=56 * 1024 * 1024),
    )(place, stay(keys), stay(values), stay(filt), stay(direct))


def turns(count):
    return [0, 1] + sorted(range(2, count), key=lambda d: (d & 1 and bin(d >> 1).count("1") == 1, -bin(d >> 1).count("1"), d))


def swap(arrays):
    count = len(arrays)
    pairs = [[(i, i ^ d) for i in range(count)] for d in turns(count)]
    return [arrays[0]] + [lax.ppermute(arrays[j], "ctx", pairs[j]) for j in range(1, count)]


def forward_kernel(ahead_ref, *refs):
    for j, x in enumerate(refs[:-1]):
        refs[-1][j] = jnp.dot(ahead_ref[...], split3(x[...]), preferred_element_type=F32)


def forward(xs, ahead):
    rows, width = xs[0].shape
    whole = pl.BlockSpec(memory_space=pltpu.VMEM)
    return pl.pallas_call(
        forward_kernel,
        in_specs=[whole] * (1 + len(xs)),
        out_specs=whole,
        out_shape=jax.ShapeDtypeStruct((len(xs), 2 * rows, width), F32),
        compiler_params=room((len(xs), 2 * rows, width), (len(xs), rows, width), (4 * rows, 3 * rows)),
    )(ahead, *xs)


def conv_kernel(place_ref, early_ref, *refs):
    first = early_ref.shape[0]
    count = (len(refs) - 6 + first) // 2
    xs, (ahead_ref, back_hbm) = refs[: count - first], refs[count - first : count - first + 2]
    outs, (spec_ref, mix_ref, back_ref, back_sem) = refs[count - first + 2 : -4], refs[-4:]
    back_in = pltpu.make_async_copy(back_hbm, back_ref, back_sem)
    back_in.start()
    rows, width = xs[0].shape
    chans = width // 2
    place = place_ref[0]

    order = turns(count)
    for j, turn in enumerate(order):
        if j < first:
            spec_ref[turn ^ place] = early_ref[j]
        else:
            x = xs[j - first]
            spec_ref[turn ^ place] = jnp.dot(ahead_ref[...], split3(x[...]), preferred_element_type=F32)

    step = 8
    parity = lax.broadcasted_iota(jnp.int32, (step, chans), 0) % 2
    sign = (1 - 2 * parity).astype(F32)

    def combine(i, carry):
        real = pl.ds(pl.multiple_of(i * step, step), step)
        imag = pl.ds(pl.multiple_of(rows + i * step, step), step)
        sig = [(spec_ref[j, real, :chans], spec_ref[j, imag, :chans]) for j in range(count)]
        sums = [None] * count
        last = None
        for lag in range(count):
            here = (spec_ref[lag, real, chans:], spec_ref[lag, imag, chans:])
            c, d = here
            if last is not None:
                c, d = c - sign * last[1], d + sign * last[0]
            last = here
            for j in range(lag, count):
                a, b = sig[j - lag]
                re, im = a * c - b * d, a * d + b * c
                sums[j] = (re, im) if lag == 0 else (sums[j][0] + re, sums[j][1] + im)
        for j in range(count):
            mix_ref[j, real], mix_ref[j, imag] = sums[j]
        return carry

    lax.fori_loop(0, rows // step, combine, 0)

    back_in.wait()
    for j in range(0, count, 2):
        pair = jnp.concatenate([mix_ref[order[j] ^ place], mix_ref[order[j + 1] ^ place]], axis=1)
        part = jnp.dot(back_ref[...], split3(pair), preferred_element_type=F32)
        outs[j][...] = part[:, :chans]
        outs[j + 1][...] = part[:, chans:]


def convolve(place, xs):
    count = len(xs)
    rows, width = xs[0].shape
    chans = width // 2
    ahead, back = (jnp.asarray(table) for table in tables(rows))
    first = max(1, count - 2)
    early = forward(xs[:first], ahead)
    whole = pl.BlockSpec(memory_space=pltpu.VMEM)
    return pl.pallas_call(
        conv_kernel,
        in_specs=[pl.BlockSpec(memory_space=pltpu.SMEM)]
        + [whole] * (count - first + 2)
        + [pl.BlockSpec(memory_space=pl.ANY)],
        out_specs=[whole] * count,
        out_shape=[pltpu.VMEM((rows, chans), F32)] * count,
        scratch_shapes=[
            pltpu.VMEM((count, 2 * rows, width), F32),
            pltpu.VMEM((count, 2 * rows, chans), F32),
            pltpu.VMEM(back.shape, BF16),
            pltpu.SemaphoreType.DMA,
        ],
        compiler_params=room(
            (count, 2 * rows, width), *[(count, 2 * rows, chans)] * 2, (count, rows, width)
        ),
    )(place, early, *xs[first:], ahead, stay(back))


CHAINS = 2


def gate_kernel(place_ref, far_ref, q_hbm, *refs):
    count = len(refs) - 5
    convs, (gated_ref, first_ref), (q_ref, conv_ref, in_sem) = refs[:count], refs[count:-3], refs[-3:]
    chans = convs[0].shape[1]
    into = [pltpu.make_async_copy(q_hbm, q_ref, in_sem.at[count])]
    into += [
        pltpu.make_async_copy(conv, conv_ref.at[turn ^ place_ref[0]], in_sem.at[j])
        for j, (turn, conv) in enumerate(zip(turns(count), convs))
    ]
    for copy in into:
        copy.start()
    for copy in into:
        copy.wait()
    for group in range(count):
        cols = slice(group * chans, (group + 1) * chans)
        gated_ref[:, cols] = (q_ref[:, cols].astype(F32) * conv_ref[group]).astype(BF16)
    first_ref[...] = jnp.dot(gated_ref[...], far_ref[...], preferred_element_type=F32)


def gate(place, query, far, convs):
    rows, width = query.shape
    count = len(convs)
    here = pl.BlockSpec(memory_space=pltpu.VMEM)
    there = pl.BlockSpec(memory_space=pl.ANY)
    part = (rows, far.shape[1])
    blocks = (count,) + convs[0].shape
    return pl.pallas_call(
        gate_kernel,
        in_specs=[pl.BlockSpec(memory_space=pltpu.SMEM), here] + [there] * (1 + count),
        out_specs=[here, here],
        out_shape=[pltpu.VMEM((rows, width), BF16), pltpu.VMEM(part, F32)],
        scratch_shapes=[
            pltpu.VMEM((rows, width), BF16),
            pltpu.VMEM(blocks, F32),
            pltpu.SemaphoreType.DMA((count + 1,)),
        ],
        compiler_params=room(*[(rows, width)] * 2, far.shape, blocks, part),
    )(place, far, stay(query), *convs)


def pass_on(up, down, step, size):
    rise = [(z, z + 1) for z in range(min(step, size - 1))]
    fall = [(z, z - 1) for z in range(max(size - step, 1), size)]
    up, down = lax.optimization_barrier((up, down))
    up = lax.ppermute(up, "tp", rise)
    down = lax.ppermute(down, "tp", fall)
    return up, down


def first_step(value, size):
    place = lax.axis_index("tp")
    if size == 2:
        return pass_on(value, value, 1, size)
    got = lax.ppermute(value, "tp", [(0, 1), (size - 1, size - 2)])
    return jnp.where(place == 1, got, 0.0), jnp.where(place == size - 2, got, 0.0)


def far_end(size):
    return jnp.where(lax.axis_index("tp") == 0, size - 1, 0)


def scatter_dot(lhs, rhs, first):
    size = lax.axis_size("tp")
    place = lax.axis_index("tp")
    rows, width = first.shape
    lhs, first = lax.optimization_barrier((lhs, first))
    terms = jnp.dot(lhs, rhs, preferred_element_type=F32)

    def own(index, k):
        start = jnp.clip(index, 0, size - 1) * (width * CHAINS) + k * width
        return lax.dynamic_slice_in_dim(terms, start, width, 1)

    firsts = [first] + [own(far_end(size), k) for k in range(1, CHAINS)]
    firsts[1:], terms = lax.optimization_barrier((firsts[1:], terms))
    sums = [first_step(value, size) for value in firsts]
    for step in range(2, size):
        for k in range(CHAINS):
            up = sums[k][0] + own(place + size - step, k)
            down = sums[k][1] + own(place - size + step, k)
            up, down, terms = lax.optimization_barrier((up, down, terms))
            sums[k] = pass_on(up, down, step, size)
    out = jnp.zeros((rows, width * CHAINS), BF16)
    for k in range(CHAINS):
        part = (own(place, k) + sums[k][0] + sums[k][1]).astype(BF16)
        out = lax.dynamic_update_slice(out, part, (0, k * width))
        out, terms = lax.optimization_barrier((out, terms))
    return out


def body(query, keys, values, filt, direct, w_out):
    count = lax.axis_size("ctx")
    size = lax.axis_size("tp")
    place = lax.axis_index("ctx").reshape(1)
    xs = swap(pack(place, keys, values, filt, direct.reshape(1, -1), count))
    part = w_out.shape[1] // (size * CHAINS)
    far = lax.dynamic_slice_in_dim(w_out, far_end(size) * (part * CHAINS), part, 1)
    xs[0], far = lax.optimization_barrier((xs[0], far))
    convs = swap(convolve(place, xs))
    gated, first = gate(place, query, far, convs)
    return scatter_dot(gated, w_out, first)


def solution(mesh):
    return jax.shard_map(
        body,
        mesh=mesh,
        in_specs=(
            P("ctx", "tp"),
            P("ctx", "tp"),
            P("ctx", "tp"),
            P("ctx", "tp"),
            P("tp"),
            P("tp", None),
        ),
        out_specs=P("ctx", "tp"),
        check_vma=False,
    )
```

```python
import functools
import math

import jax
import jax.numpy as jnp
import ml_dtypes
import numpy as np
from jax import lax
from jax.experimental import pallas as pl
from jax.experimental.pallas import tpu as pltpu
from jax.sharding import PartitionSpec as P

F32 = jnp.float32
BF16 = jnp.bfloat16


def stay(array):
    return pltpu.with_memory_space_constraint(array, pltpu.MemorySpace.HBM)


def room(*shapes):
    total = 0
    for shape in shapes:
        lanes = -(-shape[-1] // 128) * 128
        total += 4 * lanes * math.prod(shape[:-1])
    return pltpu.CompilerParams(vmem_limit_bytes=total + total // 4 + 4 * 1024 * 1024)


def halves(table):
    high = table.astype(ml_dtypes.bfloat16)
    low = (table - high.astype(np.float64)).astype(ml_dtypes.bfloat16)
    return high, low


def tables(block):
    freq = 2 * np.arange(block, dtype=np.int64) + 1
    place = np.arange(block, dtype=np.int64)
    angle = 2.0 * math.pi / (4 * block) * (freq[:, None] * place[None, :] % (4 * block))
    forward = np.concatenate([np.cos(angle), -np.sin(angle)], axis=0)
    high, low = halves(forward)
    ahead = np.concatenate([high, high, low], axis=1)
    high, low = halves(forward.T / block)
    back = np.concatenate([high, high, low], axis=1)
    return ahead, back


def split3(value):
    high = value.astype(BF16)
    low = (value - high.astype(F32)).astype(BF16)
    return jnp.concatenate([high, low, high], axis=0)


def pack_kernel(place_ref, keys_ref, values_ref, filt_ref, direct_ref, *refs):
    outs, turned_ref = refs[:-1], refs[-1]
    chans = keys_ref.shape[1] // len(outs)
    origin = jnp.logical_and(place_ref[0] == 0, pl.program_id(0) == 0)
    rows = lax.broadcasted_iota(jnp.int32, (8, chans), 0)
    if chans % 128 == 0:
        for turn, out in zip(turns(len(outs)), outs):
            cols = pl.ds(pl.multiple_of((turn ^ place_ref[0]) * chans, chans), chans)
            out[:, :chans] = keys_ref[:, cols].astype(F32) * values_ref[:, cols].astype(F32)
            out[:, chans:] = filt_ref[:, cols]
            here = jnp.where(jnp.logical_and(rows == 0, origin), direct_ref[:, cols], 0.0)
            out[:8, chans:] = filt_ref[:8, cols] + here
        return
    for group in range(len(outs)):
        cols = slice(group * chans, (group + 1) * chans)
        slot = group ^ place_ref[0]
        turned_ref[slot, :, :chans] = keys_ref[:, cols].astype(F32) * values_ref[:, cols].astype(F32)
        turned_ref[slot, :, chans:] = filt_ref[:, cols]
        here = jnp.where(jnp.logical_and(rows == 0, origin), direct_ref[:, cols], 0.0)
        turned_ref[slot, :8, chans:] = filt_ref[:8, cols] + here
    for turn, out in zip(turns(len(outs)), outs):
        out[...] = turned_ref[turn]


def pack(place, keys, values, filt, direct, count):
    rows, width = keys.shape
    step = math.gcd(rows, 128)
    spec = pl.BlockSpec((step, width), lambda i: (i, 0))
    wide = 2 * width // count
    return pl.pallas_call(
        pack_kernel,
        grid=(rows // step,),
        in_specs=[pl.BlockSpec(memory_space=pltpu.SMEM), spec, spec, spec]
        + [pl.BlockSpec((1, width), lambda i: (0, 0))],
        out_specs=[pl.BlockSpec((step, wide), lambda i: (i, 0))] * count,
        out_shape=[jax.ShapeDtypeStruct((rows, wide), F32)] * count,
        scratch_shapes=[pltpu.VMEM((count, step, wide), F32)],
        compiler_params=pltpu.CompilerParams(vmem_limit_bytes=56 * 1024 * 1024),
    )(place, stay(keys), stay(values), stay(filt), stay(direct))


def turns(count):
    return [0, 1] + sorted(range(2, count), key=lambda d: (d & 1 and bin(d >> 1).count("1") == 1, -bin(d >> 1).count("1"), d))


def swap(arrays):
    count = len(arrays)
    pairs = [[(i, i ^ d) for i in range(count)] for d in turns(count)]
    return [arrays[0]] + [lax.ppermute(arrays[j], "ctx", pairs[j]) for j in range(1, count)]


def forward_kernel(ahead_ref, *refs):
    for j, x in enumerate(refs[:-1]):
        refs[-1][j] = jnp.dot(ahead_ref[...], split3(x[...]), preferred_element_type=F32)


def forward(xs, ahead):
    rows, width = xs[0].shape
    whole = pl.BlockSpec(memory_space=pltpu.VMEM)
    return pl.pallas_call(
        forward_kernel,
        in_specs=[whole] * (1 + len(xs)),
        out_specs=whole,
        out_shape=jax.ShapeDtypeStruct((len(xs), 2 * rows, width), F32),
        compiler_params=room((len(xs), 2 * rows, width), (len(xs), rows, width), (4 * rows, 3 * rows)),
    )(ahead, *xs)


def conv_kernel(place_ref, early_ref, *refs):
    first = early_ref.shape[0]
    count = (len(refs) - 6 + first) // 2
    xs, (ahead_ref, back_hbm) = refs[: count - first], refs[count - first : count - first + 2]
    outs, (spec_ref, mix_ref, back_ref, back_sem) = refs[count - first + 2 : -4], refs[-4:]
    back_in = pltpu.make_async_copy(back_hbm, back_ref, back_sem)
    back_in.start()
    rows, width = xs[0].shape
    chans = width // 2
    place = place_ref[0]

    order = turns(count)
    for j, turn in enumerate(order):
        if j < first:
            spec_ref[turn ^ place] = early_ref[j]
        else:
            x = xs[j - first]
            spec_ref[turn ^ place] = jnp.dot(ahead_ref[...], split3(x[...]), preferred_element_type=F32)

    step = 8
    parity = lax.broadcasted_iota(jnp.int32, (step, chans), 0) % 2
    sign = (1 - 2 * parity).astype(F32)

    def combine(i, carry):
        real = pl.ds(pl.multiple_of(i * step, step), step)
        imag = pl.ds(pl.multiple_of(rows + i * step, step), step)
        sig = [(spec_ref[j, real, :chans], spec_ref[j, imag, :chans]) for j in range(count)]
        sums = [None] * count
        last = None
        for lag in range(count):
            here = (spec_ref[lag, real, chans:], spec_ref[lag, imag, chans:])
            c, d = here
            if last is not None:
                c, d = c - sign * last[1], d + sign * last[0]
            last = here
            for j in range(lag, count):
                a, b = sig[j - lag]
                re, im = a * c - b * d, a * d + b * c
                sums[j] = (re, im) if lag == 0 else (sums[j][0] + re, sums[j][1] + im)
        for j in range(count):
            mix_ref[j, real], mix_ref[j, imag] = sums[j]
        return carry

    lax.fori_loop(0, rows // step, combine, 0, unroll=2)

    back_in.wait()
    for j in range(0, count, 2):
        pair = jnp.concatenate([mix_ref[order[j] ^ place], mix_ref[order[j + 1] ^ place]], axis=1)
        part = jnp.dot(back_ref[...], split3(pair), preferred_element_type=F32)
        outs[j][...] = part[:, :chans]
        outs[j + 1][...] = part[:, chans:]


def convolve(place, xs):
    count = len(xs)
    rows, width = xs[0].shape
    chans = width // 2
    ahead, back = (jnp.asarray(table) for table in tables(rows))
    first = max(1, count - 2)
    early = forward(xs[:first], ahead)
    whole = pl.BlockSpec(memory_space=pltpu.VMEM)
    return pl.pallas_call(
        conv_kernel,
        in_specs=[pl.BlockSpec(memory_space=pltpu.SMEM)]
        + [whole] * (count - first + 2)
        + [pl.BlockSpec(memory_space=pl.ANY)],
        out_specs=[whole] * count,
        out_shape=[pltpu.VMEM((rows, chans), F32)] * count,
        scratch_shapes=[
            pltpu.VMEM((count, 2 * rows, width), F32),
            pltpu.VMEM((count, 2 * rows, chans), F32),
            pltpu.VMEM(back.shape, BF16),
            pltpu.SemaphoreType.DMA,
        ],
        compiler_params=room(
            (count, 2 * rows, width), *[(count, 2 * rows, chans)] * 2, (count, rows, width)
        ),
    )(place, early, *xs[first:], ahead, stay(back))


CHAINS = 2


def gate_kernel(place_ref, far_ref, q_hbm, *refs):
    count = len(refs) - 5
    convs, (gated_ref, first_ref), (q_ref, conv_ref, in_sem) = refs[:count], refs[count:-3], refs[-3:]
    chans = convs[0].shape[1]
    into = [pltpu.make_async_copy(q_hbm, q_ref, in_sem.at[count])]
    into += [
        pltpu.make_async_copy(conv, conv_ref.at[turn ^ place_ref[0]], in_sem.at[j])
        for j, (turn, conv) in enumerate(zip(turns(count), convs))
    ]
    for copy in into:
        copy.start()
    for copy in into:
        copy.wait()
    for group in range(count):
        cols = slice(group * chans, (group + 1) * chans)
        gated_ref[:, cols] = (q_ref[:, cols].astype(F32) * conv_ref[group]).astype(BF16)
    first_ref[...] = jnp.dot(gated_ref[...], far_ref[...], preferred_element_type=F32)


def gate(place, query, far, convs):
    rows, width = query.shape
    count = len(convs)
    here = pl.BlockSpec(memory_space=pltpu.VMEM)
    there = pl.BlockSpec(memory_space=pl.ANY)
    part = (rows, far.shape[1])
    blocks = (count,) + convs[0].shape
    return pl.pallas_call(
        gate_kernel,
        in_specs=[pl.BlockSpec(memory_space=pltpu.SMEM), here] + [there] * (1 + count),
        out_specs=[here, here],
        out_shape=[pltpu.VMEM((rows, width), BF16), pltpu.VMEM(part, F32)],
        scratch_shapes=[
            pltpu.VMEM((rows, width), BF16),
            pltpu.VMEM(blocks, F32),
            pltpu.SemaphoreType.DMA((count + 1,)),
        ],
        compiler_params=room(*[(rows, width)] * 2, far.shape, blocks, part),
    )(place, far, stay(query), *convs)


def pass_on(up, down, step, size):
    rise = [(z, z + 1) for z in range(min(step, size - 1))]
    fall = [(z, z - 1) for z in range(max(size - step, 1), size)]
    up, down = lax.optimization_barrier((up, down))
    up = lax.ppermute(up, "tp", rise)
    down = lax.ppermute(down, "tp", fall)
    return up, down


def first_step(value, size):
    place = lax.axis_index("tp")
    if size == 2:
        return pass_on(value, value, 1, size)
    got = lax.ppermute(value, "tp", [(0, 1), (size - 1, size - 2)])
    return jnp.where(place == 1, got, 0.0), jnp.where(place == size - 2, got, 0.0)


def far_end(size):
    return jnp.where(lax.axis_index("tp") == 0, size - 1, 0)


def scatter_dot(lhs, rhs, first):
    size = lax.axis_size("tp")
    place = lax.axis_index("tp")
    rows, width = first.shape
    lhs, first = lax.optimization_barrier((lhs, first))
    terms = jnp.dot(lhs, rhs, preferred_element_type=F32)

    def own(index, k):
        start = jnp.clip(index, 0, size - 1) * (width * CHAINS) + k * width
        return lax.dynamic_slice_in_dim(terms, start, width, 1)

    firsts = [first] + [own(far_end(size), k) for k in range(1, CHAINS)]
    firsts[1:], terms = lax.optimization_barrier((firsts[1:], terms))
    sums = [first_step(value, size) for value in firsts]
    for step in range(2, size):
        for k in range(CHAINS):
            up = sums[k][0] + own(place + size - step, k)
            down = sums[k][1] + own(place - size + step, k)
            up, down, terms = lax.optimization_barrier((up, down, terms))
            sums[k] = pass_on(up, down, step, size)
    out = jnp.zeros((rows, width * CHAINS), BF16)
    for k in range(CHAINS):
        part = (own(place, k) + sums[k][0] + sums[k][1]).astype(BF16)
        out = lax.dynamic_update_slice(out, part, (0, k * width))
        out, terms = lax.optimization_barrier((out, terms))
    return out


def body(query, keys, values, filt, direct, w_out):
    count = lax.axis_size("ctx")
    size = lax.axis_size("tp")
    place = lax.axis_index("ctx").reshape(1)
    xs = swap(pack(place, keys, values, filt, direct.reshape(1, -1), count))
    part = w_out.shape[1] // (size * CHAINS)
    far = lax.dynamic_slice_in_dim(w_out, far_end(size) * (part * CHAINS), part, 1)
    xs[0], far = lax.optimization_barrier((xs[0], far))
    convs = swap(convolve(place, xs))
    gated, first = gate(place, query, far, convs)
    return scatter_dot(gated, w_out, first)


def solution(mesh):
    return jax.shard_map(
        body,
        mesh=mesh,
        in_specs=(
            P("ctx", "tp"),
            P("ctx", "tp"),
            P("ctx", "tp"),
            P("ctx", "tp"),
            P("tp"),
            P("tp", None),
        ),
        out_specs=P("ctx", "tp"),
        check_vma=False,
    )
```

```python
import functools
import math

import jax
import jax.numpy as jnp
import ml_dtypes
import numpy as np
from jax import lax
from jax.experimental import pallas as pl
from jax.experimental.pallas import tpu as pltpu
from jax.sharding import PartitionSpec as P

F32 = jnp.float32
BF16 = jnp.bfloat16


def stay(array):
    return pltpu.with_memory_space_constraint(array, pltpu.MemorySpace.HBM)


def room(*shapes):
    total = 0
    for shape in shapes:
        lanes = -(-shape[-1] // 128) * 128
        total += 4 * lanes * math.prod(shape[:-1])
    return pltpu.CompilerParams(vmem_limit_bytes=total + total // 4 + 4 * 1024 * 1024)


def halves(table):
    high = table.astype(ml_dtypes.bfloat16)
    low = (table - high.astype(np.float64)).astype(ml_dtypes.bfloat16)
    return high, low


def tables(block):
    freq = 2 * np.arange(block, dtype=np.int64) + 1
    place = np.arange(block, dtype=np.int64)
    angle = 2.0 * math.pi / (4 * block) * (freq[:, None] * place[None, :] % (4 * block))
    forward = np.concatenate([np.cos(angle), -np.sin(angle)], axis=0)
    high, low = halves(forward)
    ahead = np.concatenate([high, high, low], axis=1)
    high, low = halves(forward.T / block)
    back = np.concatenate([high, high, low], axis=1)
    return ahead, back


def split3(value):
    high = value.astype(BF16)
    low = (value - high.astype(F32)).astype(BF16)
    return jnp.concatenate([high, low, high], axis=0)


def pack_kernel(place_ref, keys_ref, values_ref, filt_ref, direct_ref, *refs):
    outs, turned_ref = refs[:-1], refs[-1]
    chans = keys_ref.shape[1] // len(outs)
    origin = jnp.logical_and(place_ref[0] == 0, pl.program_id(0) == 0)
    rows = lax.broadcasted_iota(jnp.int32, (8, chans), 0)
    for group in range(len(outs)):
        cols = slice(group * chans, (group + 1) * chans)
        slot = group ^ place_ref[0]
        turned_ref[slot, :, :chans] = keys_ref[:, cols].astype(F32) * values_ref[:, cols].astype(F32)
        turned_ref[slot, :, chans:] = filt_ref[:, cols]
        here = jnp.where(jnp.logical_and(rows == 0, origin), direct_ref[:, cols], 0.0)
        turned_ref[slot, :8, chans:] = filt_ref[:8, cols] + here
    for turn, out in zip(turns(len(outs)), outs):
        out[...] = turned_ref[turn]


def pack(place, keys, values, filt, direct, count):
    rows, width = keys.shape
    step = math.gcd(rows, 128)
    spec = pl.BlockSpec((step, width), lambda i: (i, 0))
    wide = 2 * width // count
    return pl.pallas_call(
        pack_kernel,
        grid=(rows // step,),
        in_specs=[pl.BlockSpec(memory_space=pltpu.SMEM), spec, spec, spec]
        + [pl.BlockSpec((1, width), lambda i: (0, 0))],
        out_specs=[pl.BlockSpec((step, wide), lambda i: (i, 0))] * count,
        out_shape=[jax.ShapeDtypeStruct((rows, wide), F32)] * count,
        scratch_shapes=[pltpu.VMEM((count, step, wide), F32)],
        compiler_params=pltpu.CompilerParams(vmem_limit_bytes=56 * 1024 * 1024),
    )(place, stay(keys), stay(values), stay(filt), stay(direct))


def turns(count):
    return [0, 1] + sorted(range(2, count), key=lambda d: (d & 1 and bin(d >> 1).count("1") == 1, -bin(d >> 1).count("1"), d))


def swap(arrays):
    count = len(arrays)
    pairs = [[(i, i ^ d) for i in range(count)] for d in turns(count)]
    return [arrays[0]] + [lax.ppermute(arrays[j], "ctx", pairs[j]) for j in range(1, count)]


def forward_kernel(ahead_ref, *refs):
    for j, x in enumerate(refs[:-1]):
        refs[-1][j] = jnp.dot(ahead_ref[...], split3(x[...]), preferred_element_type=F32)


def forward(xs, ahead):
    rows, width = xs[0].shape
    whole = pl.BlockSpec(memory_space=pltpu.VMEM)
    return pl.pallas_call(
        forward_kernel,
        in_specs=[whole] * (1 + len(xs)),
        out_specs=whole,
        out_shape=jax.ShapeDtypeStruct((len(xs), 2 * rows, width), F32),
        compiler_params=room((len(xs), 2 * rows, width), (len(xs), rows, width), (4 * rows, 3 * rows)),
    )(ahead, *xs)


def conv_kernel(place_ref, early_ref, *refs):
    first = early_ref.shape[0]
    count = (len(refs) - 6 + first) // 2
    xs, (ahead_ref, back_hbm) = refs[: count - first], refs[count - first : count - first + 2]
    outs, (spec_ref, mix_ref, back_ref, back_sem) = refs[count - first + 2 : -4], refs[-4:]
    back_in = pltpu.make_async_copy(back_hbm, back_ref, back_sem)
    back_in.start()
    rows, width = xs[0].shape
    chans = width // 2
    place = place_ref[0]

    order = turns(count)
    for j, turn in enumerate(order):
        if j < first:
            spec_ref[turn ^ place] = early_ref[j]
        else:
            x = xs[j - first]
            spec_ref[turn ^ place] = jnp.dot(ahead_ref[...], split3(x[...]), preferred_element_type=F32)

    step = 8
    parity = lax.broadcasted_iota(jnp.int32, (step, chans), 0) % 2
    sign = (1 - 2 * parity).astype(F32)

    def combine(i, carry):
        real = pl.ds(pl.multiple_of(i * step, step), step)
        imag = pl.ds(pl.multiple_of(rows + i * step, step), step)
        sig = [(spec_ref[j, real, :chans], spec_ref[j, imag, :chans]) for j in range(count)]
        sums = [None] * count
        last = None
        for lag in range(count):
            here = (spec_ref[lag, real, chans:], spec_ref[lag, imag, chans:])
            c, d = here
            if last is not None:
                c, d = c - sign * last[1], d + sign * last[0]
            last = here
            for j in range(lag, count):
                a, b = sig[j - lag]
                re, im = a * c - b * d, a * d + b * c
                sums[j] = (re, im) if lag == 0 else (sums[j][0] + re, sums[j][1] + im)
        for j in range(count):
            mix_ref[j, real], mix_ref[j, imag] = sums[j]
        return carry

    lax.fori_loop(0, rows // step, combine, 0)

    back_in.wait()
    for j in range(0, count, 2):
        pair = jnp.concatenate([mix_ref[order[j] ^ place], mix_ref[order[j + 1] ^ place]], axis=1)
        part = jnp.dot(back_ref[...], split3(pair), preferred_element_type=F32)
        outs[j][...] = part[:, :chans]
        outs[j + 1][...] = part[:, chans:]


def convolve(place, xs):
    count = len(xs)
    rows, width = xs[0].shape
    chans = width // 2
    ahead, back = (jnp.asarray(table) for table in tables(rows))
    first = max(1, count - 2)
    early = forward(xs[:first], ahead)
    whole = pl.BlockSpec(memory_space=pltpu.VMEM)
    return pl.pallas_call(
        conv_kernel,
        in_specs=[pl.BlockSpec(memory_space=pltpu.SMEM)]
        + [whole] * (count - first + 2)
        + [pl.BlockSpec(memory_space=pl.ANY)],
        out_specs=[whole] * count,
        out_shape=[pltpu.VMEM((rows, chans), F32)] * count,
        scratch_shapes=[
            pltpu.VMEM((count, 2 * rows, width), F32),
            pltpu.VMEM((count, 2 * rows, chans), F32),
            pltpu.VMEM(back.shape, BF16),
            pltpu.SemaphoreType.DMA,
        ],
        compiler_params=room(
            (count, 2 * rows, width), *[(count, 2 * rows, chans)] * 2, (count, rows, width)
        ),
    )(place, early, *xs[first:], ahead, stay(back))


CHAINS = 2


def gate_kernel(place_ref, far_ref, q_hbm, *refs):
    count = len(refs) - 5
    convs, (gated_ref, first_ref), (q_ref, conv_ref, in_sem) = refs[:count], refs[count:-3], refs[-3:]
    chans = convs[0].shape[1]
    into = [pltpu.make_async_copy(q_hbm, q_ref, in_sem.at[count])]
    into += [
        pltpu.make_async_copy(conv, conv_ref.at[turn ^ place_ref[0]], in_sem.at[j])
        for j, (turn, conv) in enumerate(zip(turns(count), convs))
    ]
    for copy in into:
        copy.start()
    for copy in into:
        copy.wait()
    for group in range(count):
        cols = slice(group * chans, (group + 1) * chans)
        gated_ref[:, cols] = (q_ref[:, cols].astype(F32) * conv_ref[group]).astype(BF16)

    @pl.when(place_ref[1] == 1)
    def _():
        first_ref[...] = jnp.dot(gated_ref[...], far_ref[...], preferred_element_type=F32)


def gate(place, query, far, convs):
    rows, width = query.shape
    count = len(convs)
    here = pl.BlockSpec(memory_space=pltpu.VMEM)
    there = pl.BlockSpec(memory_space=pl.ANY)
    part = (rows, far.shape[1])
    blocks = (count,) + convs[0].shape
    return pl.pallas_call(
        gate_kernel,
        in_specs=[pl.BlockSpec(memory_space=pltpu.SMEM), here] + [there] * (1 + count),
        out_specs=[here, here],
        out_shape=[pltpu.VMEM((rows, width), BF16), pltpu.VMEM(part, F32)],
        scratch_shapes=[
            pltpu.VMEM((rows, width), BF16),
            pltpu.VMEM(blocks, F32),
            pltpu.SemaphoreType.DMA((count + 1,)),
        ],
        compiler_params=room(*[(rows, width)] * 2, far.shape, blocks, part),
    )(place, far, stay(query), *convs)


def pass_on(up, down, step, size):
    rise = [(z, z + 1) for z in range(min(step, size - 1))]
    fall = [(z, z - 1) for z in range(max(size - step, 1), size)]
    up, down = lax.optimization_barrier((up, down))
    up = lax.ppermute(up, "tp", rise)
    down = lax.ppermute(down, "tp", fall)
    return up, down


def first_step(value, size):
    place = lax.axis_index("tp")
    if size == 2:
        return pass_on(value, value, 1, size)
    got = lax.ppermute(value, "tp", [(0, 1), (size - 1, size - 2)])
    return jnp.where(place == 1, got, 0.0), jnp.where(place == size - 2, got, 0.0)


def far_end(size):
    return jnp.where(lax.axis_index("tp") == 0, size - 1, 0)


def scatter_dot(lhs, rhs, first):
    size = lax.axis_size("tp")
    place = lax.axis_index("tp")
    rows, width = first.shape
    lhs, first = lax.optimization_barrier((lhs, first))
    terms = jnp.dot(lhs, rhs, preferred_element_type=F32)

    def own(index, k):
        start = jnp.clip(index, 0, size - 1) * (width * CHAINS) + k * width
        return lax.dynamic_slice_in_dim(terms, start, width, 1)

    firsts = [first] + [own(far_end(size), k) for k in range(1, CHAINS)]
    firsts[1:], terms = lax.optimization_barrier((firsts[1:], terms))
    sums = [first_step(value, size) for value in firsts]
    for step in range(2, size):
        for k in range(CHAINS):
            up = sums[k][0] + own(place + size - step, k)
            down = sums[k][1] + own(place - size + step, k)
            up, down, terms = lax.optimization_barrier((up, down, terms))
            sums[k] = pass_on(up, down, step, size)
    out = jnp.zeros((rows, width * CHAINS), BF16)
    for k in range(CHAINS):
        part = (own(place, k) + sums[k][0] + sums[k][1]).astype(BF16)
        out = lax.dynamic_update_slice(out, part, (0, k * width))
        out, terms = lax.optimization_barrier((out, terms))
    return out


def body(query, keys, values, filt, direct, w_out):
    count = lax.axis_size("ctx")
    size = lax.axis_size("tp")
    place = lax.axis_index("ctx").reshape(1)
    xs = swap(pack(place, keys, values, filt, direct.reshape(1, -1), count))
    part = w_out.shape[1] // (size * CHAINS)
    far = lax.dynamic_slice_in_dim(w_out, far_end(size) * (part * CHAINS), part, 1)
    xs[0], far = lax.optimization_barrier((xs[0], far))
    convs = swap(convolve(place, xs))
    line = lax.axis_index("tp")
    ends = jnp.logical_or(line == 0, line == size - 1).astype(jnp.int32).reshape(1)
    gated, first = gate(jnp.concatenate([place, ends]), query, far, convs)
    return scatter_dot(gated, w_out, first)


def solution(mesh):
    return jax.shard_map(
        body,
        mesh=mesh,
        in_specs=(
            P("ctx", "tp"),
            P("ctx", "tp"),
            P("ctx", "tp"),
            P("ctx", "tp"),
            P("tp"),
            P("tp", None),
        ),
        out_specs=P("ctx", "tp"),
        check_vma=False,
    )
```

```python
import functools
import math

import jax
import jax.numpy as jnp
import ml_dtypes
import numpy as np
from jax import lax
from jax.experimental import pallas as pl
from jax.experimental.pallas import tpu as pltpu
from jax.sharding import PartitionSpec as P

F32 = jnp.float32
BF16 = jnp.bfloat16


def stay(array):
    return pltpu.with_memory_space_constraint(array, pltpu.MemorySpace.HBM)


def room(*shapes):
    total = 0
    for shape in shapes:
        lanes = -(-shape[-1] // 128) * 128
        total += 4 * lanes * math.prod(shape[:-1])
    return pltpu.CompilerParams(vmem_limit_bytes=total + total // 4 + 4 * 1024 * 1024)


def halves(table):
    high = table.astype(ml_dtypes.bfloat16)
    low = (table - high.astype(np.float64)).astype(ml_dtypes.bfloat16)
    return high, low


def tables(block):
    freq = 2 * np.arange(block, dtype=np.int64) + 1
    place = np.arange(block, dtype=np.int64)
    angle = 2.0 * math.pi / (4 * block) * (freq[:, None] * place[None, :] % (4 * block))
    forward = np.concatenate([np.cos(angle), -np.sin(angle)], axis=0)
    high, low = halves(forward)
    ahead = np.concatenate([high, high, low], axis=1)
    high, low = halves(forward.T / block)
    back = np.concatenate([high, high, low], axis=1)
    return ahead, back


def split3(value):
    high = value.astype(BF16)
    low = (value - high.astype(F32)).astype(BF16)
    return jnp.concatenate([high, low, high], axis=0)


def pack_kernel(place_ref, keys_ref, values_ref, filt_ref, direct_ref, *refs):
    outs, turned_ref = refs[:-1], refs[-1]
    chans = keys_ref.shape[1] // len(outs)
    origin = jnp.logical_and(place_ref[0] == 0, pl.program_id(0) == 0)
    rows = lax.broadcasted_iota(jnp.int32, (8, chans), 0)
    for group in range(len(outs)):
        cols = slice(group * chans, (group + 1) * chans)
        slot = group ^ place_ref[0]
        turned_ref[slot, :, :chans] = keys_ref[:, cols].astype(F32) * values_ref[:, cols].astype(F32)
        turned_ref[slot, :, chans:] = filt_ref[:, cols]
        here = jnp.where(jnp.logical_and(rows == 0, origin), direct_ref[:, cols], 0.0)
        turned_ref[slot, :8, chans:] = filt_ref[:8, cols] + here
    for turn, out in zip(turns(len(outs)), outs):
        out[...] = turned_ref[turn]


def pack(place, keys, values, filt, direct, count):
    rows, width = keys.shape
    step = math.gcd(rows, 128)
    spec = pl.BlockSpec((step, width), lambda i: (i, 0))
    wide = 2 * width // count
    return pl.pallas_call(
        pack_kernel,
        grid=(rows // step,),
        in_specs=[pl.BlockSpec(memory_space=pltpu.SMEM), spec, spec, spec]
        + [pl.BlockSpec((1, width), lambda i: (0, 0))],
        out_specs=[pl.BlockSpec((step, wide), lambda i: (i, 0))] * count,
        out_shape=[jax.ShapeDtypeStruct((rows, wide), F32)] * count,
        scratch_shapes=[pltpu.VMEM((count, step, wide), F32)],
        compiler_params=pltpu.CompilerParams(vmem_limit_bytes=56 * 1024 * 1024),
    )(place, stay(keys), stay(values), stay(filt), stay(direct))


def turns(count):
    return [0, 1] + sorted(range(2, count), key=lambda d: (d & 1 and bin(d >> 1).count("1") == 1, -bin(d >> 1).count("1"), d))


def swap(arrays):
    count = len(arrays)
    pairs = [[(i, i ^ d) for i in range(count)] for d in turns(count)]
    return [arrays[0]] + [lax.ppermute(arrays[j], "ctx", pairs[j]) for j in range(1, count)]


def forward_kernel(ahead_ref, *refs):
    for j, x in enumerate(refs[:-1]):
        refs[-1][j] = jnp.dot(ahead_ref[...], split3(x[...]), preferred_element_type=F32)


def forward(xs, ahead):
    rows, width = xs[0].shape
    whole = pl.BlockSpec(memory_space=pltpu.VMEM)
    return pl.pallas_call(
        forward_kernel,
        in_specs=[whole] * (1 + len(xs)),
        out_specs=whole,
        out_shape=jax.ShapeDtypeStruct((len(xs), 2 * rows, width), F32),
        compiler_params=room((len(xs), 2 * rows, width), (len(xs), rows, width), (4 * rows, 3 * rows)),
    )(ahead, *xs)


def conv_kernel(place_ref, early_ref, *refs):
    first = early_ref.shape[0]
    count = (len(refs) - 6 + first) // 2
    xs, (ahead_ref, back_hbm) = refs[: count - first], refs[count - first : count - first + 2]
    outs, (spec_ref, mix_ref, back_ref, back_sem) = refs[count - first + 2 : -4], refs[-4:]
    back_in = pltpu.make_async_copy(back_hbm, back_ref, back_sem)
    back_in.start()
    rows, width = xs[0].shape
    chans = width // 2
    place = place_ref[0]

    order = turns(count)
    for j, turn in enumerate(order):
        if j < first:
            spec_ref[turn ^ place] = early_ref[j]
        else:
            x = xs[j - first]
            spec_ref[turn ^ place] = jnp.dot(ahead_ref[...], split3(x[...]), preferred_element_type=F32)

    step = 8
    parity = lax.broadcasted_iota(jnp.int32, (step, chans), 0) % 2
    sign = (1 - 2 * parity).astype(F32)

    def combine(i, carry):
        real = pl.ds(pl.multiple_of(i * step, step), step)
        imag = pl.ds(pl.multiple_of(rows + i * step, step), step)
        sig = [(spec_ref[j, real, :chans], spec_ref[j, imag, :chans]) for j in range(count)]
        sums = [None] * count
        last = None
        for lag in range(count):
            here = (spec_ref[lag, real, chans:], spec_ref[lag, imag, chans:])
            c, d = here
            if last is not None:
                c, d = c - sign * last[1], d + sign * last[0]
            last = here
            for j in range(lag, count):
                a, b = sig[j - lag]
                re, im = a * c - b * d, a * d + b * c
                sums[j] = (re, im) if lag == 0 else (sums[j][0] + re, sums[j][1] + im)
        for j in range(count):
            mix_ref[j, real], mix_ref[j, imag] = sums[j]
        return carry

    lax.fori_loop(0, rows // step, combine, 0)

    back_in.wait()
    for j in range(0, count, 2):
        pair = jnp.concatenate([mix_ref[order[j] ^ place], mix_ref[order[j + 1] ^ place]], axis=1)
        part = jnp.dot(back_ref[...], split3(pair), preferred_element_type=F32)
        outs[j][...] = part[:, :chans]
        outs[j + 1][...] = part[:, chans:]


def convolve(place, xs):
    count = len(xs)
    rows, width = xs[0].shape
    chans = width // 2
    ahead, back = (jnp.asarray(table) for table in tables(rows))
    first = max(1, count - 2)
    early = forward(xs[:first], ahead)
    whole = pl.BlockSpec(memory_space=pltpu.VMEM)
    return pl.pallas_call(
        conv_kernel,
        in_specs=[pl.BlockSpec(memory_space=pltpu.SMEM)]
        + [whole] * (count - first + 2)
        + [pl.BlockSpec(memory_space=pl.ANY)],
        out_specs=[whole] * count,
        out_shape=[pltpu.VMEM((rows, chans), F32)] * count,
        scratch_shapes=[
            pltpu.VMEM((count, 2 * rows, width), F32),
            pltpu.VMEM((count, 2 * rows, chans), F32),
            pltpu.VMEM(back.shape, BF16),
            pltpu.SemaphoreType.DMA,
        ],
        compiler_params=room(
            (count, 2 * rows, width), *[(count, 2 * rows, chans)] * 2, (count, rows, width)
        ),
    )(place, early, *xs[first:], ahead, stay(back))


def chain_widths(width):
    first = -(-width * 5 // 8 // 128) * 128
    return [first, width - first]


def gate_kernel(place_ref, far_ref, q_hbm, *refs):
    count = len(refs) - 5
    convs, (gated_ref, first_ref), (q_ref, conv_ref, in_sem) = refs[:count], refs[count:-3], refs[-3:]
    chans = convs[0].shape[1]
    into = [pltpu.make_async_copy(q_hbm, q_ref, in_sem.at[count])]
    into += [
        pltpu.make_async_copy(conv, conv_ref.at[turn ^ place_ref[0]], in_sem.at[j])
        for j, (turn, conv) in enumerate(zip(turns(count), convs))
    ]
    for copy in into:
        copy.start()
    for copy in into:
        copy.wait()
    for group in range(count):
        cols = slice(group * chans, (group + 1) * chans)
        gated_ref[:, cols] = (q_ref[:, cols].astype(F32) * conv_ref[group]).astype(BF16)
    first_ref[...] = jnp.dot(gated_ref[...], far_ref[...], preferred_element_type=F32)


def gate(place, query, far, convs):
    rows, width = query.shape
    count = len(convs)
    here = pl.BlockSpec(memory_space=pltpu.VMEM)
    there = pl.BlockSpec(memory_space=pl.ANY)
    part = (rows, far.shape[1])
    blocks = (count,) + convs[0].shape
    return pl.pallas_call(
        gate_kernel,
        in_specs=[pl.BlockSpec(memory_space=pltpu.SMEM), here] + [there] * (1 + count),
        out_specs=[here, here],
        out_shape=[pltpu.VMEM((rows, width), BF16), pltpu.VMEM(part, F32)],
        scratch_shapes=[
            pltpu.VMEM((rows, width), BF16),
            pltpu.VMEM(blocks, F32),
            pltpu.SemaphoreType.DMA((count + 1,)),
        ],
        compiler_params=room(*[(rows, width)] * 2, far.shape, blocks, part),
    )(place, far, stay(query), *convs)


def pass_on(up, down, step, size):
    rise = [(z, z + 1) for z in range(min(step, size - 1))]
    fall = [(z, z - 1) for z in range(max(size - step, 1), size)]
    up, down = lax.optimization_barrier((up, down))
    up = lax.ppermute(up, "tp", rise)
    down = lax.ppermute(down, "tp", fall)
    return up, down


def first_step(value, size):
    place = lax.axis_index("tp")
    if size == 2:
        return pass_on(value, value, 1, size)
    got = lax.ppermute(value, "tp", [(0, 1), (size - 1, size - 2)])
    return jnp.where(place == 1, got, 0.0), jnp.where(place == size - 2, got, 0.0)


def far_end(size):
    return jnp.where(lax.axis_index("tp") == 0, size - 1, 0)


def scatter_dot(lhs, rhs, first):
    size = lax.axis_size("tp")
    place = lax.axis_index("tp")
    rows = first.shape[0]
    width = rhs.shape[1] // size
    widths = chain_widths(width)
    lhs, first = lax.optimization_barrier((lhs, first))
    terms = jnp.dot(lhs, rhs, preferred_element_type=F32)

    def own(index, k):
        start = jnp.clip(index, 0, size - 1) * width + sum(widths[:k])
        return lax.dynamic_slice_in_dim(terms, start, widths[k], 1)

    firsts = [first] + [own(far_end(size), k) for k in range(1, len(widths))]
    firsts[1:], terms = lax.optimization_barrier((firsts[1:], terms))
    sums = [first_step(value, size) for value in firsts]
    for step in range(2, size):
        for k in range(len(widths)):
            up = sums[k][0] + own(place + size - step, k)
            down = sums[k][1] + own(place - size + step, k)
            up, down, terms = lax.optimization_barrier((up, down, terms))
            sums[k] = pass_on(up, down, step, size)
    out = jnp.zeros((rows, width), BF16)
    for k in range(len(widths)):
        part = (own(place, k) + sums[k][0] + sums[k][1]).astype(BF16)
        out = lax.dynamic_update_slice(out, part, (0, sum(widths[:k])))
        out, terms = lax.optimization_barrier((out, terms))
    return out


def body(query, keys, values, filt, direct, w_out):
    count = lax.axis_size("ctx")
    size = lax.axis_size("tp")
    place = lax.axis_index("ctx").reshape(1)
    xs = swap(pack(place, keys, values, filt, direct.reshape(1, -1), count))
    part = w_out.shape[1] // size
    far = lax.dynamic_slice_in_dim(w_out, far_end(size) * part, chain_widths(part)[0], 1)
    xs[0], far = lax.optimization_barrier((xs[0], far))
    convs = swap(convolve(place, xs))
    gated, first = gate(place, query, far, convs)
    return scatter_dot(gated, w_out, first)


def solution(mesh):
    return jax.shard_map(
        body,
        mesh=mesh,
        in_specs=(
            P("ctx", "tp"),
            P("ctx", "tp"),
            P("ctx", "tp"),
            P("ctx", "tp"),
            P("tp"),
            P("tp", None),
        ),
        out_specs=P("ctx", "tp"),
        check_vma=False,
    )
```

```python
import functools
import math

import jax
import jax.numpy as jnp
import ml_dtypes
import numpy as np
from jax import lax
from jax.experimental import pallas as pl
from jax.experimental.pallas import tpu as pltpu
from jax.sharding import PartitionSpec as P

F32 = jnp.float32
BF16 = jnp.bfloat16


def stay(array):
    return pltpu.with_memory_space_constraint(array, pltpu.MemorySpace.HBM)


def room(*shapes):
    total = 0
    for shape in shapes:
        lanes = -(-shape[-1] // 128) * 128
        total += 4 * lanes * math.prod(shape[:-1])
    return pltpu.CompilerParams(vmem_limit_bytes=total + total // 4 + 4 * 1024 * 1024)


def halves(table):
    high = table.astype(ml_dtypes.bfloat16)
    low = (table - high.astype(np.float64)).astype(ml_dtypes.bfloat16)
    return high, low


def tables(block):
    freq = 2 * np.arange(block, dtype=np.int64) + 1
    place = np.arange(block, dtype=np.int64)
    angle = 2.0 * math.pi / (4 * block) * (freq[:, None] * place[None, :] % (4 * block))
    forward = np.concatenate([np.cos(angle), -np.sin(angle)], axis=0)
    high, low = halves(forward)
    ahead = np.concatenate([high, high, low], axis=1)
    high, low = halves(forward.T / block)
    back = np.concatenate([high, high, low], axis=1)
    return ahead, back


def split3(value):
    high = value.astype(BF16)
    low = (value - high.astype(F32)).astype(BF16)
    return jnp.concatenate([high, low, high], axis=0)


def pack_kernel(place_ref, keys_ref, values_ref, filt_ref, direct_ref, *refs):
    outs, turned_ref = refs[:-1], refs[-1]
    chans = keys_ref.shape[1] // len(outs)
    origin = jnp.logical_and(place_ref[0] == 0, pl.program_id(0) == 0)
    rows = lax.broadcasted_iota(jnp.int32, (8, chans), 0)
    for group in range(len(outs)):
        cols = slice(group * chans, (group + 1) * chans)
        slot = group ^ place_ref[0]
        turned_ref[slot, :, :chans] = keys_ref[:, cols].astype(F32) * values_ref[:, cols].astype(F32)
        turned_ref[slot, :, chans:] = filt_ref[:, cols]
        here = jnp.where(jnp.logical_and(rows == 0, origin), direct_ref[:, cols], 0.0)
        turned_ref[slot, :8, chans:] = filt_ref[:8, cols] + here
    for turn, out in zip(turns(len(outs)), outs):
        out[...] = turned_ref[turn]


def pack(place, keys, values, filt, direct, count):
    rows, width = keys.shape
    step = math.gcd(rows, 256)
    spec = pl.BlockSpec((step, width), lambda i: (i, 0))
    wide = 2 * width // count
    return pl.pallas_call(
        pack_kernel,
        grid=(rows // step,),
        in_specs=[pl.BlockSpec(memory_space=pltpu.SMEM), spec, spec, spec]
        + [pl.BlockSpec((1, width), lambda i: (0, 0))],
        out_specs=[pl.BlockSpec((step, wide), lambda i: (i, 0))] * count,
        out_shape=[jax.ShapeDtypeStruct((rows, wide), F32)] * count,
        scratch_shapes=[pltpu.VMEM((count, step, wide), F32)],
        compiler_params=pltpu.CompilerParams(vmem_limit_bytes=56 * 1024 * 1024),
    )(place, stay(keys), stay(values), stay(filt), stay(direct))


def turns(count):
    return [0, 1] + sorted(range(2, count), key=lambda d: (d & 1 and bin(d >> 1).count("1") == 1, -bin(d >> 1).count("1"), d))


def swap(arrays):
    count = len(arrays)
    pairs = [[(i, i ^ d) for i in range(count)] for d in turns(count)]
    return [arrays[0]] + [lax.ppermute(arrays[j], "ctx", pairs[j]) for j in range(1, count)]


def forward_kernel(ahead_ref, *refs):
    for j, x in enumerate(refs[:-1]):
        refs[-1][j] = jnp.dot(ahead_ref[...], split3(x[...]), preferred_element_type=F32)


def forward(xs, ahead):
    rows, width = xs[0].shape
    whole = pl.BlockSpec(memory_space=pltpu.VMEM)
    return pl.pallas_call(
        forward_kernel,
        in_specs=[whole] * (1 + len(xs)),
        out_specs=whole,
        out_shape=jax.ShapeDtypeStruct((len(xs), 2 * rows, width), F32),
        compiler_params=room((len(xs), 2 * rows, width), (len(xs), rows, width), (4 * rows, 3 * rows)),
    )(ahead, *xs)


def conv_kernel(place_ref, early_ref, *refs):
    first = early_ref.shape[0]
    count = (len(refs) - 6 + first) // 2
    xs, (ahead_ref, back_hbm) = refs[: count - first], refs[count - first : count - first + 2]
    outs, (spec_ref, mix_ref, back_ref, back_sem) = refs[count - first + 2 : -4], refs[-4:]
    back_in = pltpu.make_async_copy(back_hbm, back_ref, back_sem)
    back_in.start()
    rows, width = xs[0].shape
    chans = width // 2
    place = place_ref[0]

    order = turns(count)
    for j, turn in enumerate(order):
        if j < first:
            spec_ref[turn ^ place] = early_ref[j]
        else:
            x = xs[j - first]
            spec_ref[turn ^ place] = jnp.dot(ahead_ref[...], split3(x[...]), preferred_element_type=F32)

    step = 8
    parity = lax.broadcasted_iota(jnp.int32, (step, chans), 0) % 2
    sign = (1 - 2 * parity).astype(F32)

    def combine(i, carry):
        real = pl.ds(pl.multiple_of(i * step, step), step)
        imag = pl.ds(pl.multiple_of(rows + i * step, step), step)
        sig = [(spec_ref[j, real, :chans], spec_ref[j, imag, :chans]) for j in range(count)]
        sums = [None] * count
        last = None
        for lag in range(count):
            here = (spec_ref[lag, real, chans:], spec_ref[lag, imag, chans:])
            c, d = here
            if last is not None:
                c, d = c - sign * last[1], d + sign * last[0]
            last = here
            for j in range(lag, count):
                a, b = sig[j - lag]
                re, im = a * c - b * d, a * d + b * c
                sums[j] = (re, im) if lag == 0 else (sums[j][0] + re, sums[j][1] + im)
        for j in range(count):
            mix_ref[j, real], mix_ref[j, imag] = sums[j]
        return carry

    lax.fori_loop(0, rows // step, combine, 0)

    back_in.wait()
    for j in range(0, count, 2):
        pair = jnp.concatenate([mix_ref[order[j] ^ place], mix_ref[order[j + 1] ^ place]], axis=1)
        part = jnp.dot(back_ref[...], split3(pair), preferred_element_type=F32)
        outs[j][...] = part[:, :chans]
        outs[j + 1][...] = part[:, chans:]


def convolve(place, xs):
    count = len(xs)
    rows, width = xs[0].shape
    chans = width // 2
    ahead, back = (jnp.asarray(table) for table in tables(rows))
    first = max(1, count - 2)
    early = forward(xs[:first], ahead)
    whole = pl.BlockSpec(memory_space=pltpu.VMEM)
    return pl.pallas_call(
        conv_kernel,
        in_specs=[pl.BlockSpec(memory_space=pltpu.SMEM)]
        + [whole] * (count - first + 2)
        + [pl.BlockSpec(memory_space=pl.ANY)],
        out_specs=[whole] * count,
        out_shape=[pltpu.VMEM((rows, chans), F32)] * count,
        scratch_shapes=[
            pltpu.VMEM((count, 2 * rows, width), F32),
            pltpu.VMEM((count, 2 * rows, chans), F32),
            pltpu.VMEM(back.shape, BF16),
            pltpu.SemaphoreType.DMA,
        ],
        compiler_params=room(
            (count, 2 * rows, width), *[(count, 2 * rows, chans)] * 2, (count, rows, width)
        ),
    )(place, early, *xs[first:], ahead, stay(back))


CHAINS = 2


def gate_kernel(place_ref, far_ref, q_hbm, *refs):
    count = len(refs) - 5
    convs, (gated_ref, first_ref), (q_ref, conv_ref, in_sem) = refs[:count], refs[count:-3], refs[-3:]
    chans = convs[0].shape[1]
    into = [pltpu.make_async_copy(q_hbm, q_ref, in_sem.at[count])]
    into += [
        pltpu.make_async_copy(conv, conv_ref.at[turn ^ place_ref[0]], in_sem.at[j])
        for j, (turn, conv) in enumerate(zip(turns(count), convs))
    ]
    for copy in into:
        copy.start()
    for copy in into:
        copy.wait()
    for group in range(count):
        cols = slice(group * chans, (group + 1) * chans)
        gated_ref[:, cols] = (q_ref[:, cols].astype(F32) * conv_ref[group]).astype(BF16)
    first_ref[...] = jnp.dot(gated_ref[...], far_ref[...], preferred_element_type=F32)


def gate(place, query, far, convs):
    rows, width = query.shape
    count = len(convs)
    here = pl.BlockSpec(memory_space=pltpu.VMEM)
    there = pl.BlockSpec(memory_space=pl.ANY)
    part = (rows, far.shape[1])
    blocks = (count,) + convs[0].shape
    return pl.pallas_call(
        gate_kernel,
        in_specs=[pl.BlockSpec(memory_space=pltpu.SMEM), here] + [there] * (1 + count),
        out_specs=[here, here],
        out_shape=[pltpu.VMEM((rows, width), BF16), pltpu.VMEM(part, F32)],
        scratch_shapes=[
            pltpu.VMEM((rows, width), BF16),
            pltpu.VMEM(blocks, F32),
            pltpu.SemaphoreType.DMA((count + 1,)),
        ],
        compiler_params=room(*[(rows, width)] * 2, far.shape, blocks, part),
    )(place, far, stay(query), *convs)


def pass_on(up, down, step, size):
    rise = [(z, z + 1) for z in range(min(step, size - 1))]
    fall = [(z, z - 1) for z in range(max(size - step, 1), size)]
    up, down = lax.optimization_barrier((up, down))
    up = lax.ppermute(up, "tp", rise)
    down = lax.ppermute(down, "tp", fall)
    return up, down


def first_step(value, size):
    place = lax.axis_index("tp")
    if size == 2:
        return pass_on(value, value, 1, size)
    got = lax.ppermute(value, "tp", [(0, 1), (size - 1, size - 2)])
    return jnp.where(place == 1, got, 0.0), jnp.where(place == size - 2, got, 0.0)


def far_end(size):
    return jnp.where(lax.axis_index("tp") == 0, size - 1, 0)


def scatter_dot(lhs, rhs, first):
    size = lax.axis_size("tp")
    place = lax.axis_index("tp")
    rows, width = first.shape
    lhs, first = lax.optimization_barrier((lhs, first))
    terms = jnp.dot(lhs, rhs, preferred_element_type=F32)

    def own(index, k):
        start = jnp.clip(index, 0, size - 1) * (width * CHAINS) + k * width
        return lax.dynamic_slice_in_dim(terms, start, width, 1)

    firsts = [first] + [own(far_end(size), k) for k in range(1, CHAINS)]
    firsts[1:], terms = lax.optimization_barrier((firsts[1:], terms))
    sums = [first_step(value, size) for value in firsts]
    for step in range(2, size):
        for k in range(CHAINS):
            up = sums[k][0] + own(place + size - step, k)
            down = sums[k][1] + own(place - size + step, k)
            up, down, terms = lax.optimization_barrier((up, down, terms))
            sums[k] = pass_on(up, down, step, size)
    out = jnp.zeros((rows, width * CHAINS), BF16)
    for k in range(CHAINS):
        part = (own(place, k) + sums[k][0] + sums[k][1]).astype(BF16)
        out = lax.dynamic_update_slice(out, part, (0, k * width))
        out, terms = lax.optimization_barrier((out, terms))
    return out


def body(query, keys, values, filt, direct, w_out):
    count = lax.axis_size("ctx")
    size = lax.axis_size("tp")
    place = lax.axis_index("ctx").reshape(1)
    xs = swap(pack(place, keys, values, filt, direct.reshape(1, -1), count))
    part = w_out.shape[1] // (size * CHAINS)
    far = lax.dynamic_slice_in_dim(w_out, far_end(size) * (part * CHAINS), part, 1)
    xs[0], far = lax.optimization_barrier((xs[0], far))
    convs = swap(convolve(place, xs))
    gated, first = gate(place, query, far, convs)
    return scatter_dot(gated, w_out, first)


def solution(mesh):
    return jax.shard_map(
        body,
        mesh=mesh,
        in_specs=(
            P("ctx", "tp"),
            P("ctx", "tp"),
            P("ctx", "tp"),
            P("ctx", "tp"),
            P("tp"),
            P("tp", None),
        ),
        out_specs=P("ctx", "tp"),
        check_vma=False,
    )
```
